512 devices in a mesh: row: 64 (over y_lo, z, x), col: 8 (over y_hi, core).
Axes of the slice: x: 4, y: 8 (y_hi: 4, y_lo: 2; y = y_hi * 2 + y_lo), z: 8, core: 2. Of those that a mesh axis runs over, the one named last changes fastest.
Arguments:
- x_scaled: float32 [4096, 12288], P('row', 'col'), may hold values from -4 to 4
Outputs:
- update: float32 [4096, 12288], P('row', 'col')
The draws below stay inside these ranges and needn't reach their ends.
All inputs are finite; a program needn't handle non-finite values.
Results may differ from the reference program's by a relative error of at most 0.0041.
Values may be sent and summed in bfloat16 or wider, within the bound.
No kernel may reach another device: no remote copies, remote signals or barrier semaphores. Data moves between devices by JAX's collectives and lax.ppermute only.
A program may use at most 64 MiB of HBM per device.

```python
import jax
import jax.numpy as jnp
from jax import lax

M = 4096
N = 12288


def block_levels(own_key, shape, split, least, largest):
    level = 1.0
    for position, parts in split:
        draws = jax.random.uniform(jax.random.fold_in(jax.random.fold_in(own_key, 6), position), (parts,), jnp.float32, least / len(split), largest / len(split))
        level = level * jnp.repeat(jnp.exp(draws), shape[position] // parts).reshape((-1,) + (1,) * (len(shape) - 1 - position))
    return level


def bell_draw(rng, dims, width, reach, split=(), dtype=jnp.bfloat16):
    factor_of = block_levels(rng, dims, split, -0.22, 0.18) if split else 1.0
    array = jax.random.normal(rng, dims, jnp.float32) * width * factor_of
    return jnp.minimum(jnp.maximum(array, -reach), reach).astype(dtype)


def setup_inputs(seed: int = 0) -> dict:
    streams_of = jax.random.split(jax.random.key(seed), 2)
    x_scaled = bell_draw(streams_of[0], (M, N), 0.6, 4.0, ((0, 64), (1, 8)), jnp.float32)
    return dict(x_scaled=x_scaled)


coef_linear = 3.4445
coef_cubic = -4.7750
coef_quintic = 2.0315


def reference(x_scaled):
    xb = x_scaled.astype(jnp.bfloat16)
    gram = jnp.dot(xb, xb.T, preferred_element_type=jnp.float32) / N
    widened = xb.astype(jnp.float32)
    proj = jnp.dot(gram, widened, precision=lax.Precision.HIGHEST, preferred_element_type=jnp.float32)
    square = jnp.dot(proj, widened.T, precision=lax.Precision.HIGHEST, preferred_element_type=jnp.float32) / N
    poly = (coef_cubic * gram + coef_quintic * square).astype(jnp.bfloat16)
    return coef_linear * x_scaled + jnp.dot(poly, xb, preferred_element_type=jnp.float32)
```

```python
import jax
import jax.numpy as jnp
from jax import lax
from jax.sharding import Mesh, PartitionSpec as P

N = 12288

coef_linear = 3.4445
coef_cubic = -4.775
coef_quintic = 2.0315

LO = ("y_lo", "x")
COL = ("y_hi", "core")
ROW = ("y_lo", "z", "x")
EVERY = ("y_lo", "z", "x", "y_hi", "core")


def dot_nt(a, b):
    return lax.dot_general(a, b, (((1,), (1,)), ((), ())), preferred_element_type=jnp.float32)


def swap_lo_col():
    pairs = []
    for y_lo in range(2):
        for z in range(8):
            for x in range(4):
                for c in range(8):
                    to_y, to_x = divmod(c, 4)
                    source = ((y_lo * 8 + z) * 4 + x) * 8 + c
                    target = ((to_y * 8 + z) * 4 + to_x) * 8 + y_lo * 4 + x
                    pairs.append((source, target))
    return pairs


def spread(block, axis):
    return lax.all_to_all(jnp.broadcast_to(block[None], (8,) + block.shape), axis, 0, 0)


def sum_pieces(pieces, axis):
    me = lax.axis_index(axis)
    arrived = lax.all_to_all(pieces.astype(jnp.bfloat16), axis, 0, 0)
    own = lax.dynamic_index_in_dim(pieces, me, 0, keepdims=False)
    other = jnp.where(jnp.arange(8)[:, None, None] == me, 0.0, arrived.astype(jnp.float32))
    return own + other.sum(0)


def per_device(x_scaled):
    rows, cols = x_scaled.shape
    xb = x_scaled.astype(jnp.bfloat16)
    by_hi = lax.all_gather(xb, "z", axis=0, tiled=True)
    by_lo = spread(xb, LO).reshape(8 * rows, cols)

    tile = dot_nt(by_lo, by_hi) * (1.0 / N)
    gram = sum_pieces(tile.reshape(8, rows, 8 * rows), COL)

    rounded = gram.astype(jnp.bfloat16)
    left = lax.all_gather(rounded, COL, axis=0, tiled=True)
    right = spread(rounded, "z").reshape(8 * rows, 8 * rows)
    square = sum_pieces(dot_nt(left, right).reshape(8, rows, 8 * rows), LO)
    square = lax.ppermute(square, EVERY, swap_lo_col())

    poly = (coef_cubic * gram + coef_quintic * square).astype(jnp.bfloat16)
    poly = lax.all_gather(poly, COL, axis=0, tiled=True)
    product = jnp.dot(poly, by_hi, preferred_element_type=jnp.float32)
    return coef_linear * x_scaled + sum_pieces(product.reshape(8, rows, cols), LO)


def solution(mesh):
    fine = Mesh(mesh.devices.reshape(2, 8, 4, 4, 2), EVERY)
    return jax.shard_map(
        per_device,
        mesh=fine,
        in_specs=(P(ROW, COL),),
        out_specs=P(ROW, COL),
        check_vma=False,
    )
```

```python
import jax
import jax.numpy as jnp
from jax import lax
from jax.sharding import Mesh, PartitionSpec as P

N = 12288

coef_linear = 3.4445
coef_cubic = -4.775
coef_quintic = 2.0315

LO = ("y_lo", "x")
COL = ("y_hi", "core")
ROW = ("y_lo", "z", "x")
EVERY = ("y_lo", "z", "x", "y_hi", "core")


def dot_nt(a, b):
    return lax.dot_general(a, b, (((1,), (1,)), ((), ())), preferred_element_type=jnp.float32)


def swap_lo_col():
    pairs = []
    for y_lo in range(2):
        for z in range(8):
            for x in range(4):
                for c in range(8):
                    to_y, to_x = divmod(c, 4)
                    source = ((y_lo * 8 + z) * 4 + x) * 8 + c
                    target = ((to_y * 8 + z) * 4 + to_x) * 8 + y_lo * 4 + x
                    pairs.append((source, target))
    return pairs


def spread(block, axis):
    return lax.all_to_all(jnp.broadcast_to(block[None], (8,) + block.shape), axis, 0, 0)


def sum_pieces(pieces, axis):
    me = lax.axis_index(axis)
    arrived = lax.all_to_all(pieces.astype(jnp.bfloat16), axis, 0, 0)
    own = lax.dynamic_index_in_dim(pieces, me, 0, keepdims=False)
    other = jnp.where(jnp.arange(8)[:, None, None] == me, 0.0, arrived.astype(jnp.float32))
    return own + other.sum(0)


def per_device(x_scaled):
    rows, cols = x_scaled.shape
    xb = x_scaled.astype(jnp.bfloat16)
    by_hi = spread(xb, "z").reshape(8 * rows, cols)
    pair = lax.all_gather(xb, "y_lo", axis=0)
    by_lo = [lax.all_gather(pair[y], "x", axis=0, tiled=True) for y in range(2)]

    tile = jnp.concatenate([dot_nt(part, by_hi) for part in by_lo]) * (1.0 / N)
    gram = sum_pieces(tile.reshape(8, rows, 8 * rows), COL)

    rounded = gram.astype(jnp.bfloat16)
    left = lax.all_gather(rounded, COL, axis=0, tiled=True)
    right = spread(rounded, "z").reshape(8 * rows, 8 * rows)
    square = sum_pieces(dot_nt(left, right).reshape(8, rows, 8 * rows), LO)
    square = lax.ppermute(square, EVERY, swap_lo_col())

    poly = (coef_cubic * gram + coef_quintic * square).astype(jnp.bfloat16)
    poly = lax.all_gather(poly, COL, axis=0, tiled=True)
    product = jnp.dot(poly, by_hi, preferred_element_type=jnp.float32)
    return coef_linear * x_scaled + sum_pieces(product.reshape(8, rows, cols), LO)


def solution(mesh):
    fine = Mesh(mesh.devices.reshape(2, 8, 4, 4, 2), EVERY)
    return jax.shard_map(
        per_device,
        mesh=fine,
        in_specs=(P(ROW, COL),),
        out_specs=P(ROW, COL),
        check_vma=False,
    )
```

```python
import jax
import jax.numpy as jnp
from jax import lax
from jax.sharding import Mesh, PartitionSpec as P

N = 12288

coef_linear = 3.4445
coef_cubic = -4.775
coef_quintic = 2.0315

LO = ("y_lo", "x")
COL = ("core", "y_hi")
ROW = ("y_lo", "z", "x")
EVERY = ("y_lo", "z", "x", "y_hi", "core")


def dot_nt(a, b):
    return lax.dot_general(a, b, (((1,), (1,)), ((), ())), preferred_element_type=jnp.float32)


def swap_lo_col():
    pairs = []
    for y_lo in range(2):
        for z in range(8):
            for x in range(4):
                for y_hi in range(4):
                    for core in range(2):
                        source = (((y_lo * 8 + z) * 4 + x) * 4 + y_hi) * 2 + core
                        target = (((core * 8 + z) * 4 + y_hi) * 4 + x) * 2 + y_lo
                        pairs.append((source, target))
    return pairs


def spread(block, axis):
    return lax.all_to_all(jnp.broadcast_to(block[None], (8,) + block.shape), axis, 0, 0)


def sum_pieces(pieces, axis):
    me, count = lax.axis_index(axis), pieces.shape[0]
    arrived = lax.all_to_all(pieces.astype(jnp.bfloat16), axis, 0, 0)
    own = lax.dynamic_index_in_dim(pieces, me, 0, keepdims=False)
    other = jnp.where(jnp.arange(count)[:, None, None] == me, 0.0, arrived.astype(jnp.float32))
    return own + other.sum(0)


def per_device(x_scaled):
    rows, cols = x_scaled.shape
    xb = x_scaled.astype(jnp.bfloat16)
    by_hi = spread(xb, "z").reshape(8 * rows, cols)
    pair = lax.all_gather(xb, "y_lo", axis=0)
    by_lo = [lax.all_gather(pair[y], "x", axis=0, tiled=True) for y in range(2)]

    core = lax.axis_index("core")
    away = dot_nt(jnp.where(core == 0, by_lo[1], by_lo[0]), by_hi) * (1.0 / N)
    home = dot_nt(jnp.where(core == 0, by_lo[0], by_lo[1]), by_hi) * (1.0 / N)
    home = home + lax.ppermute(away, "core", [(0, 1), (1, 0)])
    gram = sum_pieces(home.reshape(4, rows, 8 * rows), "y_hi")

    rounded = gram.astype(jnp.bfloat16)
    left = lax.all_gather(rounded, COL, axis=0, tiled=True)
    right = spread(rounded, "z").reshape(8 * rows, 8 * rows)
    square = sum_pieces(dot_nt(left, right).reshape(8, rows, 8 * rows), LO)
    square = lax.ppermute(square, EVERY, swap_lo_col())

    poly = (coef_cubic * gram + coef_quintic * square).astype(jnp.bfloat16)
    poly = lax.all_gather(poly, COL, axis=0, tiled=True)
    product = jnp.dot(poly, by_hi, preferred_element_type=jnp.float32)
    return coef_linear * x_scaled + sum_pieces(product.reshape(8, rows, cols), LO)


def solution(mesh):
    fine = Mesh(mesh.devices.reshape(2, 8, 4, 4, 2), EVERY)
    return jax.shard_map(
        per_device,
        mesh=fine,
        in_specs=(P(ROW, ("y_hi", "core")),),
        out_specs=P(ROW, ("y_hi", "core")),
        check_vma=False,
    )
```

```python
import jax
import jax.numpy as jnp
from jax import lax
from jax.sharding import Mesh, PartitionSpec as P

N = 12288

coef_linear = 3.4445
coef_cubic = -4.775
coef_quintic = 2.0315

LO = ("x", "y_lo")
COL = ("y_hi", "core")
ROW = ("y_lo", "z", "x")
EVERY = ("y_lo", "z", "x", "y_hi", "core")


def dot_nt(a, b):
    return lax.dot_general(a, b, (((1,), (1,)), ((), ())), preferred_element_type=jnp.float32)


def swap_lo_col():
    pairs = []
    for y_lo in range(2):
        for z in range(8):
            for x in range(4):
                for y_hi in range(4):
                    for core in range(2):
                        source = (((y_lo * 8 + z) * 4 + x) * 4 + y_hi) * 2 + core
                        target = (((core * 8 + z) * 4 + y_hi) * 4 + x) * 2 + y_lo
                        pairs.append((source, target))
    return pairs


def spread(block, axis):
    return lax.all_to_all(jnp.broadcast_to(block[None], (8,) + block.shape), axis, 0, 0)


def sum_pieces(pieces, axis):
    me, count = lax.axis_index(axis), pieces.shape[0]
    arrived = lax.all_to_all(pieces.astype(jnp.bfloat16), axis, 0, 0)
    own = lax.dynamic_index_in_dim(pieces, me, 0, keepdims=False)
    other = jnp.where(jnp.arange(count)[:, None, None] == me, 0.0, arrived.astype(jnp.float32))
    return own + other.sum(0)


def per_device(x_scaled):
    rows, cols = x_scaled.shape
    xb = x_scaled.astype(jnp.bfloat16)
    by_hi = spread(xb, "z").reshape(8 * rows, cols)
    pair = lax.all_gather(xb, "y_lo", axis=0)
    by_lo = [lax.all_gather(pair[y], "x", axis=0, tiled=True) for y in range(2)]

    core = lax.axis_index("core")
    away = dot_nt(jnp.where(core == 0, by_lo[1], by_lo[0]), by_hi) * (1.0 / N)
    home = dot_nt(jnp.where(core == 0, by_lo[0], by_lo[1]), by_hi) * (1.0 / N)
    home = home + lax.ppermute(away, "core", [(0, 1), (1, 0)])
    gram = sum_pieces(home.reshape(4, rows, 8 * rows), "y_hi")

    rounded = gram.astype(jnp.bfloat16)
    left = lax.all_gather(rounded, COL, axis=0, tiled=True)
    right = spread(rounded, "z").reshape(8 * rows, 8 * rows)
    square = sum_pieces(dot_nt(left, right).reshape(8, rows, 8 * rows), LO)
    square = lax.ppermute(square, EVERY, swap_lo_col())

    poly = (coef_cubic * gram + coef_quintic * square).astype(jnp.bfloat16)
    poly = lax.all_gather(poly, COL, axis=0, tiled=True)
    product = jnp.dot(poly, by_hi, preferred_element_type=jnp.float32)
    return coef_linear * x_scaled + sum_pieces(product.reshape(8, rows, cols), LO)


def solution(mesh):
    fine = Mesh(mesh.devices.reshape(2, 8, 4, 4, 2), EVERY)
    return jax.shard_map(
        per_device,
        mesh=fine,
        in_specs=(P(ROW, COL),),
        out_specs=P(ROW, COL),
        check_vma=False,
    )
```

```python
import jax
import jax.numpy as jnp
from jax import lax
from jax.sharding import Mesh, PartitionSpec as P

N = 12288

coef_linear = 3.4445
coef_cubic = -4.775
coef_quintic = 2.0315

LO = ("x", "y_lo")
COL = ("y_hi", "core")
ROW = ("y_lo", "z", "x")
EVERY = ("y_lo", "z", "x", "y_hi", "core")


def dot_nt(a, b):
    return lax.dot_general(a, b, (((1,), (1,)), ((), ())), preferred_element_type=jnp.float32)


def pairs_to(place):
    pairs = []
    for y_lo in range(2):
        for z in range(8):
            for x in range(4):
                for y_hi in range(4):
                    for core in range(2):
                        to_lo, to_x, to_hi, to_core = place(y_lo, x, y_hi, core)
                        source = (((y_lo * 8 + z) * 4 + x) * 4 + y_hi) * 2 + core
                        target = (((to_lo * 8 + z) * 4 + to_x) * 4 + to_hi) * 2 + to_core
                        pairs.append((source, target))
    return pairs


def swap_lo_col(block):
    return lax.ppermute(block, EVERY, pairs_to(lambda y_lo, x, y_hi, core: (core, y_hi, x, y_lo)))


def swap_y_lo_core(block):
    return lax.ppermute(block, EVERY, pairs_to(lambda y_lo, x, y_hi, core: (core, x, y_hi, y_lo)))


def from_x(block, step):
    return lax.ppermute(block, "x", [(i, (i - step) % 4) for i in range(4)])


def spread(block, axis):
    return lax.all_to_all(jnp.broadcast_to(block[None], (8,) + block.shape), axis, 0, 0)


def sum_pieces(pieces, axis):
    me, count = lax.axis_index(axis), pieces.shape[0]
    arrived = lax.all_to_all(pieces.astype(jnp.bfloat16), axis, 0, 0)
    own = lax.dynamic_index_in_dim(pieces, me, 0, keepdims=False)
    other = jnp.where(jnp.arange(count)[:, None, None] == me, 0.0, arrived.astype(jnp.float32))
    return own + other.sum(0)


def per_device(x_scaled):
    rows, cols = x_scaled.shape
    xb = x_scaled.astype(jnp.bfloat16)
    by_hi = spread(xb, "z").reshape(8 * rows, cols)
    pair = lax.all_gather(xb, "y_lo", axis=0)
    by_lo = [lax.all_gather(pair[y], "x", axis=0, tiled=True) for y in range(2)]

    core = lax.axis_index("core")
    away = dot_nt(jnp.where(core == 0, by_lo[1], by_lo[0]), by_hi) * (1.0 / N)
    home = dot_nt(jnp.where(core == 0, by_lo[0], by_lo[1]), by_hi) * (1.0 / N)
    home = home + lax.ppermute(away, "core", [(0, 1), (1, 0)])
    gram = sum_pieces(home.reshape(4, rows, 8 * rows), "y_hi")

    depth = by_hi.shape[0]
    ahead, behind = from_x(by_hi, 1), from_x(by_hi, -1)
    across = from_x(ahead[: depth // 2], 1), from_x(behind[depth // 2 :], -1)

    rounded = gram.astype(jnp.bfloat16)
    left = lax.all_gather(rounded, COL, axis=0, tiled=True)
    right = spread(rounded, "z").reshape(8 * rows, 8 * rows)
    gram = swap_lo_col(gram)
    square = sum_pieces(dot_nt(left, right).reshape(8, rows, 8 * rows), LO)

    poly = swap_y_lo_core((coef_cubic * gram + coef_quintic * square).astype(jnp.bfloat16))
    poly = lax.all_gather(poly, COL, axis=0).reshape(4, 2, rows, depth)
    x_at, y_at = lax.axis_index("x"), lax.axis_index("y_lo")

    def product(y):
        def at(step):
            return lax.dynamic_slice(poly, ((x_at + step) % 4, y, 0, 0), (1, 1, rows, depth))[0, 0]

        def times(a, b):
            return jnp.dot(a, b, preferred_element_type=jnp.float32)

        far = at(2)
        return (
            times(at(0), by_hi) + times(at(1), ahead) + times(at(3), behind)
            + times(far[:, : depth // 2], across[0]) + times(far[:, depth // 2 :], across[1])
        )

    away = lax.ppermute(product(1 - y_at).astype(jnp.bfloat16), "y_lo", [(0, 1), (1, 0)])
    return coef_linear * x_scaled + product(y_at) + away.astype(jnp.float32)


def solution(mesh):
    fine = Mesh(mesh.devices.reshape(2, 8, 4, 4, 2), EVERY)
    return jax.shard_map(
        per_device,
        mesh=fine,
        in_specs=(P(ROW, COL),),
        out_specs=P(ROW, COL),
        check_vma=False,
    )
```

```python
import jax
import jax.numpy as jnp
from jax import lax
from jax.sharding import Mesh, PartitionSpec as P

N = 12288

coef_linear = 3.4445
coef_cubic = -4.775
coef_quintic = 2.0315

LO = ("x", "y_lo")
COL = ("y_hi", "core")
ROW = ("y_lo", "z", "x")
MESH = ("y_lo", "z", "x", "y_hi", "core")


def dot_nt(a, b):
    return lax.dot_general(a, b, (((1,), (1,)), ((), ())), preferred_element_type=jnp.float32)


def swap_x_y_hi(block):
    pairs = [((x * 4 + y) * 2 + k, (y * 4 + x) * 2 + k) for x in range(4) for y in range(4) for k in range(2)]
    return lax.ppermute(block, ("x", "y_hi", "core"), pairs)


def spread(block, axis):
    return lax.all_to_all(jnp.broadcast_to(block[None], (8,) + block.shape), axis, 0, 0)


def sum_pieces(pieces, axis):
    me, count = lax.axis_index(axis), pieces.shape[0]
    arrived = lax.all_to_all(pieces.astype(jnp.bfloat16), axis, 0, 0)
    own = lax.dynamic_index_in_dim(pieces, me, 0, keepdims=False)
    other = jnp.where(jnp.arange(count)[:, None, None] == me, 0.0, arrived.astype(jnp.float32))
    return own + other.sum(0)


def per_device(x_scaled):
    rows, cols = x_scaled.shape
    xb = x_scaled.astype(jnp.bfloat16)
    by_hi = spread(xb, "z").reshape(8 * rows, cols)
    pair = lax.all_gather(xb, "y_lo", axis=0)
    by_lo = [lax.all_gather(pair[y], "x", axis=0, tiled=True) for y in range(2)]

    core = lax.axis_index("core")
    away = dot_nt(jnp.where(core == 0, by_lo[1], by_lo[0]), by_hi) * (1.0 / N)
    home = dot_nt(jnp.where(core == 0, by_lo[0], by_lo[1]), by_hi) * (1.0 / N)
    home = home + lax.ppermute(away, "core", [(0, 1), (1, 0)])
    gram = sum_pieces(home.reshape(4, rows, 8 * rows), "y_hi")

    rounded = gram.astype(jnp.bfloat16)
    right = spread(rounded, "z").reshape(8 * rows, 8 * rows)
    right_other = lax.ppermute(right, "core", [(0, 1), (1, 0)])
    left = lax.all_gather(swap_x_y_hi(rounded), "y_lo", axis=0)
    left = lax.all_gather(left, "x", axis=0).reshape(4, 2, rows, 8 * rows)
    own = jnp.where(core == 0, left[:, 0], left[:, 1]).reshape(4 * rows, 8 * rows)
    other = jnp.where(core == 0, left[:, 1], left[:, 0]).reshape(4 * rows, 8 * rows)
    square = jnp.dot(own, right, preferred_element_type=jnp.float32) + jnp.dot(
        other, right_other, preferred_element_type=jnp.float32
    )
    square = sum_pieces(square.reshape(4, rows, 8 * rows), "y_hi")

    poly = (coef_cubic * gram + coef_quintic * square).astype(jnp.bfloat16)
    poly = lax.all_gather(poly, COL, axis=0, tiled=True)
    product = jnp.dot(poly, by_hi, preferred_element_type=jnp.float32)
    return coef_linear * x_scaled + sum_pieces(product.reshape(8, rows, cols), LO)


def solution(mesh):
    fine = Mesh(mesh.devices.reshape(2, 8, 4, 4, 2), MESH)
    return jax.shard_map(
        per_device,
        mesh=fine,
        in_specs=(P(ROW, COL),),
        out_specs=P(ROW, COL),
        check_vma=False,
    )
```

```python
import jax
import jax.numpy as jnp
from jax import lax
from jax.sharding import Mesh, PartitionSpec as P

N = 12288

coef_linear = 3.4445
coef_cubic = -4.775
coef_quintic = 2.0315

LO = ("x", "y_lo")
COL = ("y_hi", "core")
ROW = ("y_lo", "z", "x")
MESH = ("y_lo", "z", "x", "y_hi", "core")


def rest_of(x):
    return x - lax.reduce_precision(x, exponent_bits=8, mantissa_bits=7)


def dot_nt(a, b):
    return lax.dot_general(a, b, (((1,), (1,)), ((), ())), preferred_element_type=jnp.float32)


def swap_x_y_hi(block):
    pairs = [((x * 4 + y) * 2 + k, (y * 4 + x) * 2 + k) for x in range(4) for y in range(4) for k in range(2)]
    return lax.ppermute(block, ("x", "y_hi", "core"), pairs)


def spread(block, axis):
    return lax.all_to_all(jnp.broadcast_to(block[None], (8,) + block.shape), axis, 0, 0)


def sum_others(arrived, me):
    total = 0.0
    for i in range(arrived.shape[0]):
        total = total + jnp.where(i == me, 0.0, arrived[i].astype(jnp.float32))
    return total


def sum_pieces(pieces, rides, axis):
    me = lax.axis_index(axis)
    count, rows, cols = pieces.shape
    sent = jnp.concatenate([pieces, jnp.broadcast_to(rides[:, None], (count, 16, cols))], axis=1)
    arrived = lax.all_to_all(sent.astype(jnp.bfloat16), axis, 0, 0)
    own = lax.dynamic_index_in_dim(pieces, me, 0, keepdims=False)
    return own + sum_others(arrived[:, :rows], me), arrived[:, rows].astype(jnp.float32)


def per_device(x_scaled):
    rows, cols = x_scaled.shape
    xb = x_scaled.astype(jnp.bfloat16)
    by_hi = spread(xb, "z").reshape(8 * rows, cols)
    pair = lax.all_gather(xb, "y_lo", axis=0)
    by_lo = [lax.all_gather(pair[y], "x", axis=0, tiled=True) for y in range(2)]

    core = lax.axis_index("core")
    away = dot_nt(jnp.where(core == 0, by_lo[1], by_lo[0]), by_hi) * (1.0 / N)
    home = dot_nt(jnp.where(core == 0, by_lo[0], by_lo[1]), by_hi) * (1.0 / N)
    home = home + lax.ppermute(away, "core", [(0, 1), (1, 0)])
    home = home.reshape(4, rows, 8 * rows)

    x_at, y_lo_at, y_hi_at = (lax.axis_index(name) for name in ("x", "y_lo", "y_hi"))
    across = lax.broadcasted_iota(jnp.int32, (rows, 8 * rows), 1)
    down = lax.broadcasted_iota(jnp.int32, (rows, 8 * rows), 0)
    on_diagonal = across == lax.axis_index("z") * rows + down
    piece = lax.dynamic_index_in_dim(home, x_at, 0, keepdims=False)
    rest = jnp.where(on_diagonal, rest_of(piece), 0.0).sum(0)
    rides = jnp.where((jnp.arange(4)[:, None] == x_at) & (core == y_lo_at), rest[None], 0.0)
    gram, rides = sum_pieces(home, rides, "y_hi")
    gram = gram + jnp.where(on_diagonal, sum_others(rides, y_hi_at)[None], 0.0)

    rounded = gram.astype(jnp.bfloat16)
    right = spread(rounded, "z").reshape(8 * rows, 8 * rows)
    right_other = lax.ppermute(right, "core", [(0, 1), (1, 0)])
    left = lax.all_gather(swap_x_y_hi(rounded), "y_lo", axis=0)
    left = lax.all_gather(left, "x", axis=0).reshape(4, 2, rows, 8 * rows)
    own = jnp.where(core == 0, left[:, 0], left[:, 1]).reshape(4 * rows, 8 * rows)
    other = jnp.where(core == 0, left[:, 1], left[:, 0]).reshape(4 * rows, 8 * rows)
    square = jnp.dot(own, right, preferred_element_type=jnp.float32) + jnp.dot(
        other, right_other, preferred_element_type=jnp.float32
    )
    at_home = lax.dynamic_slice(left, (y_hi_at, core, 0, 0), (1, 1, rows, 8 * rows))[0, 0]
    diagonal_down = jnp.where(on_diagonal, at_home.astype(jnp.float32), 0.0).sum(1, keepdims=True)
    same = jnp.where(core == y_lo_at, right, right_other).astype(jnp.float32)
    diagonal_across = (same * jnp.eye(8 * rows, dtype=jnp.float32)).sum(0)
    rides = jnp.broadcast_to(jnp.where(y_hi_at == x_at, diagonal_across, 0.0)[None], (4, 8 * rows))
    square, rides = sum_pieces(square.reshape(4, rows, 8 * rows), rides, "y_hi")
    square = square + rest_of(gram) * (diagonal_down + rides.sum(0)[None])

    poly = (coef_cubic * gram + coef_quintic * square).astype(jnp.bfloat16)
    poly = lax.all_gather(poly, COL, axis=0, tiled=True)
    me = lax.axis_index(LO)
    product = jnp.dot(poly, by_hi, preferred_element_type=jnp.float32).astype(jnp.bfloat16)
    arrived = lax.all_to_all(product.reshape(8, rows, cols), LO, 0, 0)
    mine = lax.dynamic_slice_in_dim(poly, me * rows, rows)
    own = jnp.dot(mine, by_hi, preferred_element_type=jnp.float32)
    return coef_linear * x_scaled + own + sum_others(arrived, me)


def solution(mesh):
    fine = Mesh(mesh.devices.reshape(2, 8, 4, 4, 2), MESH)
    return jax.shard_map(
        per_device,
        mesh=fine,
        in_specs=(P(ROW, COL),),
        out_specs=P(ROW, COL),
        check_vma=False,
    )
```

```python
import jax
import jax.numpy as jnp
from jax import lax
from jax.sharding import Mesh, PartitionSpec as P

N = 12288

coef_linear = 3.4445
coef_cubic = -4.775
coef_quintic = 2.0315

LO = ("x", "y_lo")
COL = ("y_hi", "core")
ROW = ("y_lo", "z", "x")
MESH = ("y_lo", "z", "x", "y_hi", "core")


def rest_of(x):
    return x - lax.reduce_precision(x, exponent_bits=8, mantissa_bits=7)


def dot_nt(a, b):
    return lax.dot_general(a, b, (((1,), (1,)), ((), ())), preferred_element_type=jnp.float32)


def swap_x_y_hi(block):
    pairs = [((x * 4 + y) * 2 + k, (y * 4 + x) * 2 + k) for x in range(4) for y in range(4) for k in range(2)]
    return lax.ppermute(block, ("x", "y_hi", "core"), pairs)


def spread(block, axis):
    return lax.all_to_all(jnp.broadcast_to(block[None], (8,) + block.shape), axis, 0, 0)


def sum_others(arrived, me):
    total = 0.0
    for i in range(arrived.shape[0]):
        total = total + jnp.where(i == me, 0.0, arrived[i].astype(jnp.float32))
    return total


def sum_pieces(pieces, axis):
    me = lax.axis_index(axis)
    arrived = lax.all_to_all(pieces.astype(jnp.bfloat16), axis, 0, 0)
    return lax.dynamic_index_in_dim(pieces, me, 0, keepdims=False) + sum_others(arrived, me)


def per_device(x_scaled):
    rows, cols = x_scaled.shape
    xb = x_scaled.astype(jnp.bfloat16)
    by_hi = spread(xb, "z").reshape(8 * rows, cols)
    pair = lax.all_gather(xb, "y_lo", axis=0)
    by_lo = [lax.all_gather(pair[y], "x", axis=0, tiled=True) for y in range(2)]

    tile = jnp.concatenate([dot_nt(part, by_hi) for part in by_lo]) * (1.0 / N)
    gram = sum_pieces(tile.reshape(8, rows, 8 * rows), ("core", "y_hi"))

    rounded = gram.astype(jnp.bfloat16)
    right = spread(rounded, "z").reshape(8 * rows, 8 * rows)
    right_other = lax.ppermute(right, "core", [(0, 1), (1, 0)])
    left = lax.all_gather(swap_x_y_hi(rounded), "y_lo", axis=0)
    left = lax.all_gather(left, "x", axis=0).reshape(4, 2, rows, 8 * rows)
    core = lax.axis_index("core")
    own = jnp.where(core == 0, left[:, 0], left[:, 1]).reshape(4 * rows, 8 * rows)
    other = jnp.where(core == 0, left[:, 1], left[:, 0]).reshape(4 * rows, 8 * rows)
    square = jnp.dot(own, right, preferred_element_type=jnp.float32) + jnp.dot(
        other, right_other, preferred_element_type=jnp.float32
    )
    square = sum_pieces(square.reshape(4, rows, 8 * rows), "y_hi")

    at_home = lax.dynamic_slice(left, (lax.axis_index("y_hi"), core, 0, 0), (1, 1, rows, 8 * rows))[0, 0]
    column = lax.broadcasted_iota(jnp.int32, at_home.shape, 1) - lax.axis_index("z") * rows
    on_diagonal = column == lax.broadcasted_iota(jnp.int32, at_home.shape, 0)
    diagonal = jnp.where(on_diagonal, at_home.astype(jnp.float32), 0.0).sum(1, keepdims=True)
    square = square + rest_of(gram) * (2.0 * diagonal)

    poly = (coef_cubic * gram + coef_quintic * square).astype(jnp.bfloat16)
    poly = lax.all_gather(poly, COL, axis=0, tiled=True)
    me = lax.axis_index(LO)
    product = jnp.dot(poly, by_hi, preferred_element_type=jnp.float32).astype(jnp.bfloat16)
    arrived = lax.all_to_all(product.reshape(8, rows, cols), LO, 0, 0)
    mine = lax.dynamic_slice_in_dim(poly, me * rows, rows)
    own = jnp.dot(mine, by_hi, preferred_element_type=jnp.float32)
    return coef_linear * x_scaled + own + sum_others(arrived, me)


def solution(mesh):
    fine = Mesh(mesh.devices.reshape(2, 8, 4, 4, 2), MESH)
    return jax.shard_map(
        per_device,
        mesh=fine,
        in_specs=(P(ROW, COL),),
        out_specs=P(ROW, COL),
        check_vma=False,
    )
```

```python
import jax
import jax.numpy as jnp
from jax import lax
from jax.sharding import Mesh, PartitionSpec as P

N = 12288

coef_linear = 3.4445
coef_cubic = -4.775
coef_quintic = 2.0315

LO = ("x", "y_lo")
COL = ("y_hi", "core")
ROW = ("y_lo", "z", "x")
MESH = ("y_lo", "z", "x", "y_hi", "core")


def rest_of(x):
    return x - lax.reduce_precision(x, exponent_bits=8, mantissa_bits=7)


def dot_nt(a, b):
    return lax.dot_general(a, b, (((1,), (1,)), ((), ())), preferred_element_type=jnp.float32)


def swap_x_y_hi(block):
    pairs = [((x * 4 + y) * 2 + k, (y * 4 + x) * 2 + k) for x in range(4) for y in range(4) for k in range(2)]
    return lax.ppermute(block, ("x", "y_hi", "core"), pairs)


def spread(block, axis):
    return lax.all_to_all(jnp.broadcast_to(block[None], (8,) + block.shape), axis, 0, 0)


def sum_others(arrived, me):
    total = 0.0
    for i in range(arrived.shape[0]):
        total = total + jnp.where(i == me, 0.0, arrived[i].astype(jnp.float32))
    return total


def sum_pieces(pieces, axis):
    me = lax.axis_index(axis)
    arrived = lax.all_to_all(pieces.astype(jnp.bfloat16), axis, 0, 0)
    return lax.dynamic_index_in_dim(pieces, me, 0, keepdims=False) + sum_others(arrived, me)


def per_device(x_scaled):
    rows, cols = x_scaled.shape
    by_hi = spread(x_scaled.astype(jnp.bfloat16), "z").reshape(8 * rows, cols)
    xb = lax.reduce_precision(x_scaled, exponent_bits=8, mantissa_bits=7).astype(jnp.bfloat16)
    pair = lax.all_gather(xb, "y_lo", axis=0)
    by_lo = [lax.all_gather(pair[y], "x", axis=0, tiled=True) for y in range(2)]

    tile = jnp.concatenate([dot_nt(part, by_hi) for part in by_lo]) * (1.0 / N)
    gram = sum_pieces(tile.reshape(8, rows, 8 * rows), ("core", "y_hi"))

    rounded = gram.astype(jnp.bfloat16)
    right = spread(rounded, "z").reshape(8 * rows, 8 * rows)
    right_other = lax.ppermute(right, "core", [(0, 1), (1, 0)])
    left = lax.all_gather(swap_x_y_hi(rounded), "x", axis=0)
    left = lax.all_gather(left, "y_lo", axis=0)
    core = lax.axis_index("core")
    own = jnp.where(core == 0, left[0], left[1]).reshape(4 * rows, 8 * rows)
    other = jnp.where(core == 0, left[1], left[0]).reshape(4 * rows, 8 * rows)
    square = jnp.dot(own, right, preferred_element_type=jnp.float32) + jnp.dot(
        other, right_other, preferred_element_type=jnp.float32
    )
    square = sum_pieces(square.reshape(4, rows, 8 * rows), "y_hi")

    at_home = lax.dynamic_slice(left, (core, lax.axis_index("y_hi"), 0, 0), (1, 1, rows, 8 * rows))[0, 0]
    column = lax.broadcasted_iota(jnp.int32, at_home.shape, 1) - lax.axis_index("z") * rows
    on_diagonal = column == lax.broadcasted_iota(jnp.int32, at_home.shape, 0)
    diagonal = jnp.where(on_diagonal, at_home.astype(jnp.float32), 0.0).sum(1, keepdims=True)
    square = square + rest_of(gram) * (2.0 * diagonal)

    poly = (coef_cubic * gram + coef_quintic * square).astype(jnp.bfloat16)
    poly = lax.all_gather(poly, COL, axis=0, tiled=True)
    me = lax.axis_index(LO)
    product = jnp.dot(poly, by_hi, preferred_element_type=jnp.float32).astype(jnp.bfloat16)
    arrived = lax.all_to_all(product.reshape(8, rows, cols), LO, 0, 0)
    mine = lax.dynamic_slice_in_dim(poly, me * rows, rows)
    own = jnp.dot(mine, by_hi, preferred_element_type=jnp.float32)
    return coef_linear * x_scaled + own + sum_others(arrived, me)


def solution(mesh):
    fine = Mesh(mesh.devices.reshape(2, 8, 4, 4, 2), MESH)
    return jax.shard_map(
        per_device,
        mesh=fine,
        in_specs=(P(ROW, COL),),
        out_specs=P(ROW, COL),
        check_vma=False,
    )
```

```python
import jax
import jax.numpy as jnp
from jax import lax
from jax.sharding import Mesh, PartitionSpec as P

N = 12288

coef_linear = 3.4445
coef_cubic = -4.775
coef_quintic = 2.0315

LO = ("x", "y_lo")
COL = ("y_hi", "core")
ROW = ("y_lo", "z", "x")
MESH = ("y_lo", "z", "x", "y_hi", "core")


def rest_of(x):
    return x - lax.reduce_precision(x, exponent_bits=8, mantissa_bits=7)


def dot_nt(a, b):
    return lax.dot_general(a, b, (((1,), (1,)), ((), ())), preferred_element_type=jnp.float32)


def swap_x_y_hi(block):
    pairs = [((x * 4 + y) * 2 + k, (y * 4 + x) * 2 + k) for x in range(4) for y in range(4) for k in range(2)]
    return lax.ppermute(block, ("x", "y_hi", "core"), pairs)


def swap_lo_col(block):
    pairs = []
    for y_lo in range(2):
        for z in range(8):
            for x in range(4):
                for y_hi in range(4):
                    for core in range(2):
                        source = (((y_lo * 8 + z) * 4 + x) * 4 + y_hi) * 2 + core
                        target = (((core * 8 + z) * 4 + y_hi) * 4 + x) * 2 + y_lo
                        pairs.append((source, target))
    return lax.ppermute(block, MESH, pairs)


def spread(block, axis):
    return lax.all_to_all(jnp.broadcast_to(block[None], (8,) + block.shape), axis, 0, 0)


def sum_others(arrived, me):
    total = 0.0
    for i in range(arrived.shape[0]):
        total = total + jnp.where(i == me, 0.0, arrived[i].astype(jnp.float32))
    return total


def sum_pieces(pieces, axis):
    me = lax.axis_index(axis)
    arrived = lax.all_to_all(pieces.astype(jnp.bfloat16), axis, 0, 0)
    return lax.dynamic_index_in_dim(pieces, me, 0, keepdims=False) + sum_others(arrived, me)


def per_device(x_scaled):
    rows, cols = x_scaled.shape
    xb = x_scaled.astype(jnp.bfloat16)
    by_hi = spread(xb, "z").reshape(8 * rows, cols)
    pair = lax.all_gather(xb, "y_lo", axis=0)
    by_lo = [lax.all_gather(pair[y], "x", axis=0, tiled=True) for y in range(2)]

    tile = jnp.concatenate([dot_nt(part, by_hi) for part in by_lo]) * (1.0 / N)
    gram = sum_pieces(tile.reshape(8, rows, 8 * rows), ("core", "y_hi"))

    rounded = gram.astype(jnp.bfloat16)
    right = spread(rounded, "z").reshape(8 * rows, 8 * rows)
    left = lax.all_gather(rounded, COL, axis=0, tiled=True)
    by_hi_pair = lax.ppermute(by_hi, "y_lo", [(0, 1), (1, 0)])
    gram = swap_lo_col(gram)
    square = sum_pieces(dot_nt(left, right).reshape(8, rows, 8 * rows), LO)

    at_home = lax.dynamic_slice_in_dim(left, lax.axis_index(LO) * rows, rows)
    column = lax.broadcasted_iota(jnp.int32, at_home.shape, 1) - lax.axis_index("z") * rows
    on_diagonal = column == lax.broadcasted_iota(jnp.int32, at_home.shape, 0)
    diagonal = jnp.where(on_diagonal, at_home.astype(jnp.float32), 0.0).sum(1, keepdims=True)
    square = square + rest_of(gram) * (2.0 * diagonal)

    poly = swap_x_y_hi((coef_cubic * gram + coef_quintic * square).astype(jnp.bfloat16))
    poly = lax.all_gather(poly, COL, axis=0).reshape(4, 2, rows, 8 * rows)
    y_lo = lax.axis_index("y_lo")
    near = jnp.where(y_lo == 0, poly[:, 0], poly[:, 1]).reshape(4 * rows, 8 * rows)
    far = jnp.where(y_lo == 0, poly[:, 1], poly[:, 0]).reshape(4 * rows, 8 * rows)
    product = jnp.dot(near, by_hi, preferred_element_type=jnp.float32) + jnp.dot(
        far, by_hi_pair, preferred_element_type=jnp.float32
    )
    return coef_linear * x_scaled + sum_pieces(product.reshape(4, rows, cols), "x")


def solution(mesh):
    fine = Mesh(mesh.devices.reshape(2, 8, 4, 4, 2), MESH)
    return jax.shard_map(
        per_device,
        mesh=fine,
        in_specs=(P(ROW, COL),),
        out_specs=P(ROW, COL),
        check_vma=False,
    )
```

```python
import jax
import jax.numpy as jnp
from jax import lax
from jax.sharding import Mesh, PartitionSpec as P

N = 12288

coef_linear = 3.4445
coef_cubic = -4.775
coef_quintic = 2.0315

LO = ("x", "y_lo")
COL = ("y_hi", "core")
ROW = ("y_lo", "z", "x")
MESH = ("y_lo", "z", "x", "y_hi", "core")


def dot_nt(a, b):
    return lax.dot_general(a, b, (((1,), (1,)), ((), ())), preferred_element_type=jnp.float32)


def rest_of(x):
    return x - lax.reduce_precision(x, exponent_bits=8, mantissa_bits=7)


def swap_lo_col(block):
    pairs = []
    for y_lo in range(2):
        for z in range(8):
            for x in range(4):
                for y_hi in range(4):
                    for core in range(2):
                        source = (((y_lo * 8 + z) * 4 + x) * 4 + y_hi) * 2 + core
                        target = (((core * 8 + z) * 4 + y_hi) * 4 + x) * 2 + y_lo
                        pairs.append((source, target))
    return lax.ppermute(block, MESH, pairs)


def spread(block, axis):
    return lax.all_to_all(jnp.broadcast_to(block[None], (8,) + block.shape), axis, 0, 0)


def sum_pieces(pieces, axis):
    me = lax.axis_index(axis)
    mine = jnp.arange(pieces.shape[0])[:, None, None] == me
    arrived = lax.all_to_all(jnp.where(mine, 0.0, pieces).astype(jnp.bfloat16), axis, 0, 0)
    own = lax.dynamic_index_in_dim(pieces, me, 0, keepdims=False)
    return own + arrived.astype(jnp.float32).sum(0)


def per_device(x_scaled):
    rows, cols = x_scaled.shape
    xb = x_scaled.astype(jnp.bfloat16)
    by_hi = spread(xb, "z").reshape(8 * rows, cols)
    pair = lax.all_gather(xb, "y_lo", axis=0)
    by_lo = jnp.concatenate([lax.all_gather(pair[y], "x", axis=0, tiled=True) for y in range(2)])

    tile = dot_nt(by_lo, by_hi) * (1.0 / N)
    gram = sum_pieces(tile.reshape(8, rows, 8 * rows), ("core", "y_hi"))

    rounded = gram.astype(jnp.bfloat16)
    left = lax.all_gather(rounded, COL, axis=0, tiled=True)
    right = spread(rounded, "z").reshape(8 * rows, 8 * rows)
    square = sum_pieces(dot_nt(left, right).reshape(8, rows, 8 * rows), LO)

    at_home = lax.dynamic_slice_in_dim(left, lax.axis_index(LO) * rows, rows)
    column = lax.broadcasted_iota(jnp.int32, at_home.shape, 1) - lax.axis_index("z") * rows
    on_diagonal = column == lax.broadcasted_iota(jnp.int32, at_home.shape, 0)
    diagonal = jnp.where(on_diagonal, at_home.astype(jnp.float32), 0.0).sum(1, keepdims=True)
    moved = swap_lo_col(jnp.concatenate([square, jnp.broadcast_to(diagonal, (rows, 128))], axis=1))
    square, diagonal = moved[:, : 8 * rows], moved[:, 8 * rows : 8 * rows + 1]

    square = square + rest_of(gram) * (2.0 * diagonal)
    poly = (coef_cubic * gram + coef_quintic * square).astype(jnp.bfloat16)
    poly = lax.all_gather(poly, COL, axis=0, tiled=True)
    product = jnp.dot(poly, by_hi, preferred_element_type=jnp.float32)
    return coef_linear * x_scaled + sum_pieces(product.reshape(8, rows, cols), LO)


def solution(mesh):
    fine = Mesh(mesh.devices.reshape(2, 8, 4, 4, 2), MESH)
    return jax.shard_map(
        per_device,
        mesh=fine,
        in_specs=(P(ROW, COL),),
        out_specs=P(ROW, COL),
        check_vma=False,
    )
```

```python
import jax
import jax.numpy as jnp
from jax import lax
from jax.sharding import Mesh, PartitionSpec as P

N = 12288

coef_linear = 3.4445
coef_cubic = -4.775
coef_quintic = 2.0315

LO = ("x", "y_lo")
COL = ("y_hi", "core")
ROW = ("y_lo", "z", "x")
MESH = ("y_lo", "z", "x", "y_hi", "core")


def rest_of(x):
    return x - lax.reduce_precision(x, exponent_bits=8, mantissa_bits=7)


def dot_nt(a, b):
    return lax.dot_general(a, b, (((1,), (1,)), ((), ())), preferred_element_type=jnp.float32)


def swap_x_y_hi(block):
    pairs = [((x * 4 + y) * 2 + k, (y * 4 + x) * 2 + k) for x in range(4) for y in range(4) for k in range(2)]
    return lax.ppermute(block, ("x", "y_hi", "core"), pairs)


def spread(block, axis):
    return lax.all_to_all(jnp.broadcast_to(block[None], (8,) + block.shape), axis, 0, 0)


def sum_pieces(pieces, axis):
    me = lax.axis_index(axis)
    mine = jnp.arange(pieces.shape[0])[:, None, None] == me
    arrived = lax.all_to_all(jnp.where(mine, 0.0, pieces).astype(jnp.bfloat16), axis, 0, 0)
    own = lax.dynamic_index_in_dim(pieces, me, 0, keepdims=False)
    return own + arrived.astype(jnp.float32).sum(0)


def per_device(x_scaled):
    rows, cols = x_scaled.shape
    xb = x_scaled.astype(jnp.bfloat16)
    by_hi = spread(xb, "z").reshape(8 * rows, cols)
    pair = lax.all_gather(xb, "y_lo", axis=0)
    by_lo = [lax.all_gather(pair[y], "x", axis=0, tiled=True) for y in range(2)]

    tile = jnp.concatenate([dot_nt(part, by_hi) for part in by_lo]) * (1.0 / N)
    gram = sum_pieces(tile.reshape(8, rows, 8 * rows), ("core", "y_hi"))

    rounded = gram.astype(jnp.bfloat16)
    right = spread(rounded, "z").reshape(8 * rows, 8 * rows)
    right_other = lax.ppermute(right, "core", [(0, 1), (1, 0)])
    left = lax.all_gather(swap_x_y_hi(rounded), "y_lo", axis=0)
    left = lax.all_gather(left, "x", axis=0).reshape(4, 2, rows, 8 * rows)
    core = lax.axis_index("core")
    own = jnp.where(core == 0, left[:, 0], left[:, 1]).reshape(4 * rows, 8 * rows)
    other = jnp.where(core == 0, left[:, 1], left[:, 0]).reshape(4 * rows, 8 * rows)
    square = jnp.dot(own, right, preferred_element_type=jnp.float32) + jnp.dot(
        other, right_other, preferred_element_type=jnp.float32
    )
    square = sum_pieces(square.reshape(4, rows, 8 * rows), "y_hi")

    at_home = lax.dynamic_slice(left, (lax.axis_index("y_hi"), core, 0, 0), (1, 1, rows, 8 * rows))[0, 0]
    column = lax.broadcasted_iota(jnp.int32, at_home.shape, 1) - lax.axis_index("z") * rows
    on_diagonal = column == lax.broadcasted_iota(jnp.int32, at_home.shape, 0)
    diagonal = jnp.where(on_diagonal, at_home.astype(jnp.float32), 0.0).sum(1, keepdims=True)
    square = square + rest_of(gram) * (2.0 * diagonal)

    poly = (coef_cubic * gram + coef_quintic * square).astype(jnp.bfloat16)
    poly = lax.all_gather(poly, COL, axis=0, tiled=True)
    product = jnp.dot(poly, by_hi, preferred_element_type=jnp.float32)
    return coef_linear * x_scaled + sum_pieces(product.reshape(8, rows, cols), LO)


def solution(mesh):
    fine = Mesh(mesh.devices.reshape(2, 8, 4, 4, 2), MESH)
    return jax.shard_map(
        per_device,
        mesh=fine,
        in_specs=(P(ROW, COL),),
        out_specs=P(ROW, COL),
        check_vma=False,
    )
```

```python
import jax
import jax.numpy as jnp
from jax import lax
from jax.sharding import Mesh, PartitionSpec as P

N = 12288

coef_linear = 3.4445
coef_cubic = -4.775
coef_quintic = 2.0315

LO = ("x", "y_lo")
COL = ("y_hi", "core")
ROW = ("y_lo", "z", "x")
MESH = ("y_lo", "z", "x", "y_hi", "core")


def rest_of(x):
    return x - lax.reduce_precision(x, exponent_bits=8, mantissa_bits=7)


def dot_nt(a, b):
    return lax.dot_general(a, b, (((1,), (1,)), ((), ())), preferred_element_type=jnp.float32)


def swap_x_y_hi(block):
    pairs = [((x * 4 + y) * 2 + k, (y * 4 + x) * 2 + k) for x in range(4) for y in range(4) for k in range(2)]
    return lax.ppermute(block, ("x", "y_hi", "core"), pairs)


def spread(block, axis):
    return lax.all_to_all(jnp.broadcast_to(block[None], (8,) + block.shape), axis, 0, 0)


def sum_pieces(pieces, axis):
    me = lax.axis_index(axis)
    mine = jnp.arange(pieces.shape[0])[:, None, None] == me
    arrived = lax.all_to_all(jnp.where(mine, 0.0, pieces).astype(jnp.bfloat16), axis, 0, 0)
    own = lax.dynamic_slice(pieces, (me, 0, 0), (1,) + pieces.shape[1:], allow_negative_indices=False)[0]
    return own + arrived.astype(jnp.float32).sum(0)


def per_device(x_scaled):
    rows, cols = x_scaled.shape
    xb = x_scaled.astype(jnp.bfloat16)
    by_hi = spread(xb, "z").reshape(8 * rows, cols)
    pair = lax.all_gather(xb, "y_lo", axis=0)
    by_lo = [lax.all_gather(pair[y], "x", axis=0, tiled=True) for y in range(2)]

    tile = jnp.concatenate([dot_nt(part, by_hi) for part in by_lo]) * (1.0 / N)
    gram = sum_pieces(tile.reshape(8, rows, 8 * rows), ("core", "y_hi"))

    rounded = gram.astype(jnp.bfloat16)
    right = spread(rounded, "z").reshape(8 * rows, 8 * rows)
    right_other = lax.ppermute(right, "core", [(0, 1), (1, 0)])
    left = lax.all_gather(swap_x_y_hi(rounded), "y_lo", axis=0)
    left = lax.all_gather(left, "x", axis=0).reshape(4, 2, rows, 8 * rows)
    core = lax.axis_index("core")
    own = jnp.where(core == 0, left[:, 0], left[:, 1]).reshape(4 * rows, 8 * rows)
    other = jnp.where(core == 0, left[:, 1], left[:, 0]).reshape(4 * rows, 8 * rows)
    square = jnp.dot(own, right, preferred_element_type=jnp.float32) + jnp.dot(
        other, right_other, preferred_element_type=jnp.float32
    )
    square = sum_pieces(square.reshape(4, rows, 8 * rows), "y_hi")

    place = (lax.axis_index("y_hi"), core, 0, 0)
    at_home = lax.dynamic_slice(left, place, (1, 1, rows, 8 * rows), allow_negative_indices=False)[0, 0]
    column = lax.broadcasted_iota(jnp.int32, at_home.shape, 1) - lax.axis_index("z") * rows
    on_diagonal = column == lax.broadcasted_iota(jnp.int32, at_home.shape, 0)
    diagonal = jnp.where(on_diagonal, at_home.astype(jnp.float32), 0.0).sum(1, keepdims=True)
    square = square + rest_of(gram) * (2.0 * diagonal)

    poly = (coef_cubic * gram + coef_quintic * square).astype(jnp.bfloat16)
    poly = lax.all_gather(poly, COL, axis=0, tiled=True)
    product = jnp.dot(poly, by_hi, preferred_element_type=jnp.float32)
    return coef_linear * x_scaled + sum_pieces(product.reshape(8, rows, cols), LO)


def solution(mesh):
    fine = Mesh(mesh.devices.reshape(2, 8, 4, 4, 2), MESH)
    return jax.shard_map(
        per_device,
        mesh=fine,
        in_specs=(P(ROW, COL),),
        out_specs=P(ROW, COL),
        check_vma=False,
    )
```

```python
import jax
import jax.numpy as jnp
from jax import lax
from jax.sharding import Mesh, PartitionSpec as P

N = 12288

coef_linear = 3.4445
coef_cubic = -4.775
coef_quintic = 2.0315

LO = ("x", "y_lo")
COL = ("y_hi", "core")
ROW = ("y_lo", "z", "x")
MESH = ("y_lo", "z", "x", "y_hi", "core")


def rest_of(x):
    return x - lax.reduce_precision(x, exponent_bits=8, mantissa_bits=7)


def dot_nt(a, b):
    return lax.dot_general(a, b, (((1,), (1,)), ((), ())), preferred_element_type=jnp.float32)


def swap_x_y_hi(block):
    pairs = [((x * 4 + y) * 2 + k, (y * 4 + x) * 2 + k) for x in range(4) for y in range(4) for k in range(2)]
    return lax.ppermute(block, ("x", "y_hi", "core"), pairs)


def spread(block, axis):
    return lax.all_to_all(jnp.broadcast_to(block[None], (8,) + block.shape), axis, 0, 0)


def sum_pieces(pieces, axis):
    me = lax.axis_index(axis)
    mine = jnp.arange(pieces.shape[0])[:, None, None] == me
    arrived = lax.all_to_all(jnp.where(mine, 0.0, pieces).astype(jnp.bfloat16), axis, 0, 0)
    own = lax.dynamic_slice(pieces, (me, 0, 0), (1,) + pieces.shape[1:], allow_negative_indices=False)[0]
    return own + arrived.astype(jnp.float32).sum(0)


def per_device(x_scaled):
    rows, cols = x_scaled.shape
    xb = x_scaled.astype(jnp.bfloat16)
    by_hi = spread(xb, "z").reshape(8 * rows, cols)
    pair = lax.all_gather(xb, "y_lo", axis=0)
    by_lo = [lax.all_gather(pair[y], "x", axis=0, tiled=True) for y in range(2)]

    tile = jnp.concatenate([dot_nt(part, by_hi) for part in by_lo]) * (1.0 / N)
    gram = sum_pieces(tile.reshape(8, rows, 8 * rows), ("core", "y_hi"))

    rounded = gram.astype(jnp.bfloat16)
    moved = swap_x_y_hi(rounded)
    left = lax.all_gather(moved, "y_lo", axis=0)
    left = lax.all_gather(left, "x", axis=0).reshape(4, 2, rows, 8 * rows)
    right = spread(rounded + 0 * moved[:1, :1], "z").reshape(8 * rows, 8 * rows)
    right_other = lax.ppermute(right, "core", [(0, 1), (1, 0)])
    core = lax.axis_index("core")
    own = jnp.where(core == 0, left[:, 0], left[:, 1]).reshape(4 * rows, 8 * rows)
    other = jnp.where(core == 0, left[:, 1], left[:, 0]).reshape(4 * rows, 8 * rows)
    square = jnp.dot(own, right, preferred_element_type=jnp.float32) + jnp.dot(
        other, right_other, preferred_element_type=jnp.float32
    )
    square = sum_pieces(square.reshape(4, rows, 8 * rows), "y_hi")

    place = (lax.axis_index("y_hi"), core, 0, 0)
    at_home = lax.dynamic_slice(left, place, (1, 1, rows, 8 * rows), allow_negative_indices=False)[0, 0]
    column = lax.broadcasted_iota(jnp.int32, at_home.shape, 1) - lax.axis_index("z") * rows
    on_diagonal = column == lax.broadcasted_iota(jnp.int32, at_home.shape, 0)
    diagonal = jnp.where(on_diagonal, at_home.astype(jnp.float32), 0.0).sum(1, keepdims=True)
    square = square + rest_of(gram) * (2.0 * diagonal)

    poly = (coef_cubic * gram + coef_quintic * square).astype(jnp.bfloat16)
    poly = lax.all_gather(poly, COL, axis=0, tiled=True)
    product = jnp.dot(poly, by_hi, preferred_element_type=jnp.float32)
    return coef_linear * x_scaled + sum_pieces(product.reshape(8, rows, cols), LO)


def solution(mesh):
    fine = Mesh(mesh.devices.reshape(2, 8, 4, 4, 2), MESH)
    return jax.shard_map(
        per_device,
        mesh=fine,
        in_specs=(P(ROW, COL),),
        out_specs=P(ROW, COL),
        check_vma=False,
    )
```

```python
import jax
import jax.numpy as jnp
from jax import lax
from jax.sharding import Mesh, PartitionSpec as P

N = 12288

coef_linear = 3.4445
coef_cubic = -4.775
coef_quintic = 2.0315

LO = ("x", "y_lo")
COL = ("y_hi", "core")
ROW = ("y_lo", "z", "x")
MESH = ("y_lo", "z", "x", "y_hi", "core")


def dot_nt(a, b):
    return lax.dot_general(a, b, (((1,), (1,)), ((), ())), preferred_element_type=jnp.float32)


def rest_of(x):
    return x - lax.reduce_precision(x, exponent_bits=8, mantissa_bits=7)


def swap_lo_col(block):
    pairs = []
    for y_lo in range(2):
        for z in range(8):
            for x in range(4):
                for y_hi in range(4):
                    for core in range(2):
                        source = (((y_lo * 8 + z) * 4 + x) * 4 + y_hi) * 2 + core
                        target = (((core * 8 + z) * 4 + y_hi) * 4 + x) * 2 + y_lo
                        pairs.append((source, target))
    return lax.ppermute(block, MESH, pairs)


def spread(block, axis):
    return lax.all_to_all(jnp.broadcast_to(block[None], (8,) + block.shape), axis, 0, 0)


def sum_pieces(pieces, axis):
    me = lax.axis_index(axis)
    mine = jnp.arange(pieces.shape[0])[:, None, None] == me
    arrived = lax.all_to_all(jnp.where(mine, 0.0, pieces).astype(jnp.bfloat16), axis, 0, 0)
    own = lax.dynamic_slice(pieces, (me, 0, 0), (1,) + pieces.shape[1:], allow_negative_indices=False)[0]
    return own + arrived.astype(jnp.float32).sum(0)


def per_device(x_scaled):
    rows, cols = x_scaled.shape
    xb = x_scaled.astype(jnp.bfloat16)
    by_hi = spread(xb, "z").reshape(8 * rows, cols)
    pair = lax.all_gather(xb, "y_lo", axis=0)
    by_lo = [lax.all_gather(pair[y], "x", axis=0, tiled=True) for y in range(2)]

    tile = jnp.concatenate([dot_nt(part, by_hi) for part in by_lo]) * (1.0 / N)
    gram = sum_pieces(tile.reshape(8, rows, 8 * rows), ("core", "y_hi"))

    rounded = gram.astype(jnp.bfloat16)
    left = lax.all_gather(rounded, COL, axis=0, tiled=True)
    right = spread(rounded, "z").reshape(8 * rows, 8 * rows)
    square = sum_pieces(dot_nt(left, right).reshape(8, rows, 8 * rows), LO)

    place = (lax.axis_index(LO) * rows, 0)
    at_home = lax.dynamic_slice(left, place, (rows, 8 * rows), allow_negative_indices=False)
    column = lax.broadcasted_iota(jnp.int32, at_home.shape, 1) - lax.axis_index("z") * rows
    on_diagonal = column == lax.broadcasted_iota(jnp.int32, at_home.shape, 0)
    diagonal = jnp.where(on_diagonal, at_home.astype(jnp.float32), 0.0).sum(0, keepdims=True)
    moved = swap_lo_col(jnp.concatenate([square, jnp.broadcast_to(diagonal, (8, 8 * rows))]))
    square, diagonal = moved[:rows], jnp.where(on_diagonal, moved[rows : rows + 1], 0.0).sum(1, keepdims=True)

    square = square + rest_of(gram) * (2.0 * diagonal)
    poly = (coef_cubic * gram + coef_quintic * square).astype(jnp.bfloat16)
    poly = lax.all_gather(poly, COL, axis=0, tiled=True)
    product = jnp.dot(poly, by_hi, preferred_element_type=jnp.float32)
    return coef_linear * x_scaled + sum_pieces(product.reshape(8, rows, cols), LO)


def solution(mesh):
    fine = Mesh(mesh.devices.reshape(2, 8, 4, 4, 2), MESH)
    return jax.shard_map(
        per_device,
        mesh=fine,
        in_specs=(P(ROW, COL),),
        out_specs=P(ROW, COL),
        check_vma=False,
    )
```

```python
import jax
import jax.numpy as jnp
from jax import lax
from jax.experimental import pallas as pl
from jax.sharding import Mesh, PartitionSpec as P

N = 12288

coef_linear = 3.4445
coef_cubic = -4.775
coef_quintic = 2.0315

LO = ("x", "y_lo")
COL = ("y_hi", "core")
ROW = ("y_lo", "z", "x")
MESH = ("y_lo", "z", "x", "y_hi", "core")


def rest_of(x):
    return x - lax.reduce_precision(x, exponent_bits=8, mantissa_bits=7)


def dot_nt(a, b):
    return lax.dot_general(a, b, (((1,), (1,)), ((), ())), preferred_element_type=jnp.float32)


def swap_x_y_hi(block):
    pairs = [((x * 4 + y) * 2 + k, (y * 4 + x) * 2 + k) for x in range(4) for y in range(4) for k in range(2)]
    return lax.ppermute(block, ("x", "y_hi", "core"), pairs)


def round_and_copy(x, count):
    def body(x_ref, one_ref, copies_ref):
        block = x_ref[...].astype(jnp.bfloat16)
        one_ref[...] = block
        copies_ref[0] = block

    rows, cols = x.shape
    whole = pl.BlockSpec((rows, cols), lambda i: (0, 0))
    return pl.pallas_call(
        body,
        grid=(count,),
        in_specs=[whole],
        out_specs=[whole, pl.BlockSpec((1, rows, cols), lambda i: (i, 0, 0))],
        out_shape=[
            jax.ShapeDtypeStruct((rows, cols), jnp.bfloat16),
            jax.ShapeDtypeStruct((count, rows, cols), jnp.bfloat16),
        ],
    )(x)


def spread(block, axis):
    return lax.all_to_all(jnp.broadcast_to(block[None], (8,) + block.shape), axis, 0, 0)


def sum_pieces(pieces, axis):
    me = lax.axis_index(axis)
    mine = jnp.arange(pieces.shape[0])[:, None, None] == me
    arrived = lax.all_to_all(jnp.where(mine, 0.0, pieces).astype(jnp.bfloat16), axis, 0, 0)
    own = lax.dynamic_slice(pieces, (me, 0, 0), (1,) + pieces.shape[1:], allow_negative_indices=False)[0]
    return own + arrived.astype(jnp.float32).sum(0)


def per_device(x_scaled):
    rows, cols = x_scaled.shape
    xb, copies = round_and_copy(x_scaled, 8)
    by_hi = lax.all_to_all(copies, "z", 0, 0).reshape(8 * rows, cols)
    pair = lax.all_gather(xb, "y_lo", axis=0)
    by_lo = [lax.all_gather(pair[y], "x", axis=0, tiled=True) for y in range(2)]

    tile = jnp.concatenate([dot_nt(part, by_hi) for part in by_lo]) * (1.0 / N)
    gram = sum_pieces(tile.reshape(8, rows, 8 * rows), ("core", "y_hi"))

    rounded = gram.astype(jnp.bfloat16)
    right = spread(rounded, "z").reshape(8 * rows, 8 * rows)
    right_other = lax.ppermute(right, "core", [(0, 1), (1, 0)])
    left = lax.all_gather(swap_x_y_hi(rounded), "y_lo", axis=0)
    left = lax.all_gather(left, "x", axis=0).reshape(4, 2, rows, 8 * rows)
    core = lax.axis_index("core")
    own = jnp.where(core == 0, left[:, 0], left[:, 1]).reshape(4 * rows, 8 * rows)
    other = jnp.where(core == 0, left[:, 1], left[:, 0]).reshape(4 * rows, 8 * rows)
    square = jnp.dot(own, right, preferred_element_type=jnp.float32) + jnp.dot(
        other, right_other, preferred_element_type=jnp.float32
    )
    square = sum_pieces(square.reshape(4, rows, 8 * rows), "y_hi")

    place = (lax.axis_index("y_hi"), core, 0, 0)
    at_home = lax.dynamic_slice(left, place, (1, 1, rows, 8 * rows), allow_negative_indices=False)[0, 0]
    column = lax.broadcasted_iota(jnp.int32, at_home.shape, 1) - lax.axis_index("z") * rows
    on_diagonal = column == lax.broadcasted_iota(jnp.int32, at_home.shape, 0)
    diagonal = jnp.where(on_diagonal, at_home.astype(jnp.float32), 0.0).sum(1, keepdims=True)
    square = square + rest_of(gram) * (2.0 * diagonal)

    poly = (coef_cubic * gram + coef_quintic * square).astype(jnp.bfloat16)
    poly = lax.all_gather(poly, COL, axis=0, tiled=True)
    product = jnp.dot(poly, by_hi, preferred_element_type=jnp.float32)
    return coef_linear * x_scaled + sum_pieces(product.reshape(8, rows, cols), LO)


def solution(mesh):
    fine = Mesh(mesh.devices.reshape(2, 8, 4, 4, 2), MESH)
    return jax.shard_map(
        per_device,
        mesh=fine,
        in_specs=(P(ROW, COL),),
        out_specs=P(ROW, COL),
        check_vma=False,
    )
```

```python
import jax
import jax.numpy as jnp
from jax import lax
from jax.sharding import Mesh, PartitionSpec as P

N = 12288

coef_linear = 3.4445
coef_cubic = -4.775
coef_quintic = 2.0315

LO = ("x", "y_lo")
COL = ("y_hi", "core")
ROW = ("y_lo", "z", "x")
MESH = ("y_lo", "z", "x", "y_hi", "core")


def rest_of(x):
    return x - lax.reduce_precision(x, exponent_bits=8, mantissa_bits=7)


def dot_nt(a, b):
    return lax.dot_general(a, b, (((1,), (1,)), ((), ())), preferred_element_type=jnp.float32)


def swap_x_y_hi(block):
    pairs = [((x * 4 + y) * 2 + k, (y * 4 + x) * 2 + k) for x in range(4) for y in range(4) for k in range(2)]
    return lax.ppermute(block, ("x", "y_hi", "core"), pairs)


def spread(block, axis):
    return lax.all_to_all(jnp.broadcast_to(block[None], (8,) + block.shape), axis, 0, 0)


def sum_pieces(pieces, axis):
    me = lax.axis_index(axis)
    mine = jnp.arange(pieces.shape[0])[:, None, None] == me
    arrived = lax.all_to_all(jnp.where(mine, 0.0, pieces).astype(jnp.bfloat16), axis, 0, 0)
    own = lax.dynamic_slice(pieces, (me, 0, 0), (1,) + pieces.shape[1:], allow_negative_indices=False)[0]
    return own + arrived.astype(jnp.float32).sum(0)


def per_device(x_scaled):
    rows, cols = x_scaled.shape
    xb = x_scaled.astype(jnp.bfloat16)
    linear = lax.optimization_barrier(coef_linear * x_scaled)
    by_hi = spread(xb, "z").reshape(8 * rows, cols)
    pair = lax.all_gather(xb, "y_lo", axis=0)
    by_lo = [lax.all_gather(pair[y], "x", axis=0, tiled=True) for y in range(2)]

    tile = jnp.concatenate([dot_nt(part, by_hi) for part in by_lo]) * (1.0 / N)
    gram = sum_pieces(tile.reshape(8, rows, 8 * rows), ("core", "y_hi"))

    rounded = gram.astype(jnp.bfloat16)
    right = spread(rounded, "z").reshape(8 * rows, 8 * rows)
    right_other = lax.ppermute(right, "core", [(0, 1), (1, 0)])
    left = lax.all_gather(swap_x_y_hi(rounded), "y_lo", axis=0)
    left = lax.all_gather(left, "x", axis=0).reshape(4, 2, rows, 8 * rows)
    core = lax.axis_index("core")
    own = jnp.where(core == 0, left[:, 0], left[:, 1]).reshape(4 * rows, 8 * rows)
    other = jnp.where(core == 0, left[:, 1], left[:, 0]).reshape(4 * rows, 8 * rows)
    square = jnp.dot(own, right, preferred_element_type=jnp.float32) + jnp.dot(
        other, right_other, preferred_element_type=jnp.float32
    )
    square = sum_pieces(square.reshape(4, rows, 8 * rows), "y_hi")

    place = (lax.axis_index("y_hi"), core, 0, 0)
    at_home = lax.dynamic_slice(left, place, (1, 1, rows, 8 * rows), allow_negative_indices=False)[0, 0]
    column = lax.broadcasted_iota(jnp.int32, at_home.shape, 1) - lax.axis_index("z") * rows
    on_diagonal = column == lax.broadcasted_iota(jnp.int32, at_home.shape, 0)
    diagonal = jnp.where(on_diagonal, at_home.astype(jnp.float32), 0.0).sum(1, keepdims=True)
    square = square + rest_of(gram) * (2.0 * diagonal)

    poly = (coef_cubic * gram + coef_quintic * square).astype(jnp.bfloat16)
    poly = lax.all_gather(poly, COL, axis=0, tiled=True)
    product = jnp.dot(poly, by_hi, preferred_element_type=jnp.float32)
    return linear + sum_pieces(product.reshape(8, rows, cols), LO)


def solution(mesh):
    fine = Mesh(mesh.devices.reshape(2, 8, 4, 4, 2), MESH)
    return jax.shard_map(
        per_device,
        mesh=fine,
        in_specs=(P(ROW, COL),),
        out_specs=P(ROW, COL),
        check_vma=False,
    )
```

```python
import jax
import jax.numpy as jnp
from jax import lax
from jax.sharding import Mesh, PartitionSpec as P

N = 12288

coef_linear = 3.4445
coef_cubic = -4.775
coef_quintic = 2.0315

LO = ("x", "y_lo")
COL = ("y_hi", "core")
ROW = ("y_lo", "z", "x")
MESH = ("y_lo", "z", "x", "y_hi", "core")


def rest_of(x):
    return x - lax.reduce_precision(x, exponent_bits=8, mantissa_bits=7)


def dot_nt(a, b):
    return lax.dot_general(a, b, (((1,), (1,)), ((), ())), preferred_element_type=jnp.float32)


def swap_x_y_hi(block):
    pairs = [((x * 4 + y) * 2 + k, (y * 4 + x) * 2 + k) for x in range(4) for y in range(4) for k in range(2)]
    return lax.ppermute(block, ("x", "y_hi", "core"), pairs)


def spread(block, axis):
    count = lax.axis_size(axis)
    return lax.all_to_all(jnp.broadcast_to(block[None], (count,) + block.shape), axis, 0, 0)


def sum_pieces(pieces, axis):
    me = lax.axis_index(axis)
    mine = jnp.arange(pieces.shape[0])[:, None, None] == me
    arrived = lax.all_to_all(jnp.where(mine, 0.0, pieces).astype(jnp.bfloat16), axis, 0, 0)
    own = lax.dynamic_slice(pieces, (me, 0, 0), (1,) + pieces.shape[1:], allow_negative_indices=False)[0]
    return own + arrived.astype(jnp.float32).sum(0)


def per_device(x_scaled):
    rows, cols = x_scaled.shape
    xb = x_scaled.astype(jnp.bfloat16)
    by_hi = spread(xb, "z").reshape(8 * rows, cols)
    pair = lax.all_gather(xb, "y_lo", axis=0)
    by_lo = [lax.all_gather(pair[y], "x", axis=0, tiled=True) for y in range(2)]

    tile = jnp.concatenate([dot_nt(part, by_hi) for part in by_lo]) * (1.0 / N)
    gram = sum_pieces(tile.reshape(8, rows, 8 * rows), ("core", "y_hi"))

    rounded = gram.astype(jnp.bfloat16)
    right = spread(rounded, "z").reshape(8 * rows, 8 * rows)
    right_other = lax.ppermute(right, "core", [(0, 1), (1, 0)])
    left = lax.all_gather(swap_x_y_hi(rounded), "y_lo", axis=0)
    left = spread(left, "x")
    core = lax.axis_index("core")
    own = jnp.where(core == 0, left[:, 0], left[:, 1]).reshape(4 * rows, 8 * rows)
    other = jnp.where(core == 0, left[:, 1], left[:, 0]).reshape(4 * rows, 8 * rows)
    square = jnp.dot(own, right, preferred_element_type=jnp.float32) + jnp.dot(
        other, right_other, preferred_element_type=jnp.float32
    )
    square = sum_pieces(square.reshape(4, rows, 8 * rows), "y_hi")

    place = (lax.axis_index("y_hi"), core, 0, 0)
    at_home = lax.dynamic_slice(left, place, (1, 1, rows, 8 * rows), allow_negative_indices=False)[0, 0]
    column = lax.broadcasted_iota(jnp.int32, at_home.shape, 1) - lax.axis_index("z") * rows
    on_diagonal = column == lax.broadcasted_iota(jnp.int32, at_home.shape, 0)
    diagonal = jnp.where(on_diagonal, at_home.astype(jnp.float32), 0.0).sum(1, keepdims=True)
    square = square + rest_of(gram) * (2.0 * diagonal)

    poly = (coef_cubic * gram + coef_quintic * square).astype(jnp.bfloat16)
    poly = lax.all_gather(poly, COL, axis=0, tiled=True)
    product = jnp.dot(poly, by_hi, preferred_element_type=jnp.float32)
    return coef_linear * x_scaled + sum_pieces(product.reshape(8, rows, cols), LO)


def solution(mesh):
    fine = Mesh(mesh.devices.reshape(2, 8, 4, 4, 2), MESH)
    return jax.shard_map(
        per_device,
        mesh=fine,
        in_specs=(P(ROW, COL),),
        out_specs=P(ROW, COL),
        check_vma=False,
    )
```

```python
import jax
import jax.numpy as jnp
from jax import lax
from jax.sharding import Mesh, PartitionSpec as P

N = 12288

coef_linear = 3.4445
coef_cubic = -4.775
coef_quintic = 2.0315

LO = ("x", "y_lo")
COL = ("y_hi", "core")
ROW = ("y_lo", "z", "x")
MESH = ("y_lo", "z", "x", "y_hi", "core")


def rest_of(x):
    return x - lax.reduce_precision(x, exponent_bits=8, mantissa_bits=7)


def dot_nt(a, b):
    return lax.dot_general(a, b, (((1,), (1,)), ((), ())), preferred_element_type=jnp.float32)


def swap_x_y_hi(block):
    pairs = [((x * 4 + y) * 2 + k, (y * 4 + x) * 2 + k) for x in range(4) for y in range(4) for k in range(2)]
    return lax.ppermute(block, ("x", "y_hi", "core"), pairs)


def spread(block, axis):
    count = lax.axis_size(axis)
    return lax.all_to_all(jnp.broadcast_to(block[None], (count,) + block.shape), axis, 0, 0)


def sum_pieces(pieces, axis):
    me = lax.axis_index(axis)
    mine = jnp.arange(pieces.shape[0])[:, None, None] == me
    arrived = lax.all_to_all(jnp.where(mine, 0.0, pieces).astype(jnp.bfloat16), axis, 0, 0)
    own = lax.dynamic_slice(pieces, (me, 0, 0), (1,) + pieces.shape[1:], allow_negative_indices=False)[0]
    return own + arrived.astype(jnp.float32).sum(0)


def per_device(x_scaled):
    rows, cols = x_scaled.shape
    xb = x_scaled.astype(jnp.bfloat16)
    by_hi = spread(xb, "z").reshape(8 * rows, cols)
    pair = lax.all_gather(xb, "y_lo", axis=0)
    by_lo = [lax.all_gather(pair[y], "x", axis=0, tiled=True) for y in range(2)]

    tile = jnp.concatenate([dot_nt(part, by_hi) for part in by_lo]) * (1.0 / N)
    gram = sum_pieces(tile.reshape(8, rows, 8 * rows), ("core", "y_hi"))

    rounded = gram.astype(jnp.bfloat16)
    right = spread(rounded, "z").reshape(8 * rows, 8 * rows)
    right_other = lax.ppermute(right, "core", [(0, 1), (1, 0)])
    left = lax.all_gather(swap_x_y_hi(rounded), "y_lo", axis=0)
    core = lax.axis_index("core")
    left = jnp.concatenate(
        [jnp.where(core == 0, left[0], left[1]), jnp.where(core == 0, left[1], left[0])], axis=1
    )
    left = spread(left, "x").reshape(4 * rows, 16 * rows)
    own, other = left[:, : 8 * rows], left[:, 8 * rows :]
    square = jnp.dot(own, right, preferred_element_type=jnp.float32) + jnp.dot(
        other, right_other, preferred_element_type=jnp.float32
    )
    square = sum_pieces(square.reshape(4, rows, 8 * rows), "y_hi")

    place = (lax.axis_index("y_hi") * rows, 0)
    at_home = lax.dynamic_slice(own, place, (rows, 8 * rows), allow_negative_indices=False)
    column = lax.broadcasted_iota(jnp.int32, at_home.shape, 1) - lax.axis_index("z") * rows
    on_diagonal = column == lax.broadcasted_iota(jnp.int32, at_home.shape, 0)
    diagonal = jnp.where(on_diagonal, at_home.astype(jnp.float32), 0.0).sum(1, keepdims=True)
    square = square + rest_of(gram) * (2.0 * diagonal)

    poly = (coef_cubic * gram + coef_quintic * square).astype(jnp.bfloat16)
    poly = lax.all_gather(poly, COL, axis=0, tiled=True)
    product = jnp.dot(poly, by_hi, preferred_element_type=jnp.float32)
    return coef_linear * x_scaled + sum_pieces(product.reshape(8, rows, cols), LO)


def solution(mesh):
    fine = Mesh(mesh.devices.reshape(2, 8, 4, 4, 2), MESH)
    return jax.shard_map(
        per_device,
        mesh=fine,
        in_specs=(P(ROW, COL),),
        out_specs=P(ROW, COL),
        check_vma=False,
    )
```

```python
import jax
import jax.numpy as jnp
from jax import lax
from jax.sharding import Mesh, PartitionSpec as P

N = 12288

coef_linear = 3.4445
coef_cubic = -4.775
coef_quintic = 2.0315

LO = ("x", "y_lo")
COL = ("y_hi", "core")
ROW = ("y_lo", "z", "x")
MESH = ("y_lo", "z", "x", "y_hi", "core")


def rest_of(x):
    return x - lax.reduce_precision(x, exponent_bits=8, mantissa_bits=7)


def dot_nt(a, b):
    return lax.dot_general(a, b, (((1,), (1,)), ((), ())), preferred_element_type=jnp.float32)


def swap_x_y_hi(block):
    pairs = [((x * 4 + y) * 2 + k, (y * 4 + x) * 2 + k) for x in range(4) for y in range(4) for k in range(2)]
    return lax.ppermute(block, ("x", "y_hi", "core"), pairs)


def spread(block, axis):
    count = lax.axis_size(axis)
    return lax.all_to_all(jnp.broadcast_to(block[None], (count,) + block.shape), axis, 0, 0)


def sum_pieces(pieces, axis):
    me = lax.axis_index(axis)
    mine = jnp.arange(pieces.shape[0])[:, None, None] == me
    arrived = lax.all_to_all(jnp.where(mine, 0.0, pieces).astype(jnp.bfloat16), axis, 0, 0)
    own = lax.dynamic_slice(pieces, (me, 0, 0), (1,) + pieces.shape[1:], allow_negative_indices=False)[0]
    return own + arrived.astype(jnp.float32).sum(0)


def per_device(x_scaled):
    rows, cols = x_scaled.shape
    xb = x_scaled.astype(jnp.bfloat16)
    by_hi = spread(xb, "z").reshape(8 * rows, cols)
    pair = lax.all_gather(xb, "y_lo", axis=0)
    by_lo = [lax.all_gather(pair[y], "x", axis=0, tiled=True) for y in range(2)]

    tile = jnp.concatenate([dot_nt(part, by_hi) for part in by_lo]) * (1.0 / N)
    gram = sum_pieces(tile.reshape(8, rows, 8 * rows), ("core", "y_hi"))

    rounded = gram.astype(jnp.bfloat16)
    right = spread(rounded, "z").reshape(8 * rows, 8 * rows)
    right_other = lax.ppermute(right, "core", [(0, 1), (1, 0)])
    left = lax.all_gather(swap_x_y_hi(rounded), "y_lo", axis=0)
    left = lax.all_gather(left, "x", axis=0).reshape(4, 2, rows, 8 * rows)
    core = lax.axis_index("core")
    own = jnp.where(core == 0, left[:, 0], left[:, 1]).reshape(4 * rows, 8 * rows)
    other = jnp.where(core == 0, left[:, 1], left[:, 0]).reshape(4 * rows, 8 * rows)
    square = jnp.dot(own, right, preferred_element_type=jnp.float32) + jnp.dot(
        other, right_other, preferred_element_type=jnp.float32
    )
    square = sum_pieces(square.reshape(4, rows, 8 * rows), "y_hi")

    place = (lax.axis_index("y_hi"), core, 0, 0)
    at_home = lax.dynamic_slice(left, place, (1, 1, rows, 8 * rows), allow_negative_indices=False)[0, 0]
    column = lax.broadcasted_iota(jnp.int32, at_home.shape, 1) - lax.axis_index("z") * rows
    on_diagonal = column == lax.broadcasted_iota(jnp.int32, at_home.shape, 0)
    diagonal = jnp.where(on_diagonal, at_home.astype(jnp.float32), 0.0).sum(1, keepdims=True)
    square = square + rest_of(gram) * (2.0 * diagonal)

    poly = (coef_cubic * gram + coef_quintic * square).astype(jnp.bfloat16)
    poly = lax.all_gather(spread(poly, "y_hi"), "core", axis=0).reshape(8 * rows, 8 * rows)
    product = jnp.dot(poly, by_hi, preferred_element_type=jnp.float32)
    return coef_linear * x_scaled + sum_pieces(product.reshape(8, rows, cols), ("y_lo", "x"))


def solution(mesh):
    fine = Mesh(mesh.devices.reshape(2, 8, 4, 4, 2), MESH)
    return jax.shard_map(
        per_device,
        mesh=fine,
        in_specs=(P(ROW, COL),),
        out_specs=P(ROW, COL),
        check_vma=False,
    )
```

```python
import jax
import jax.numpy as jnp
from jax import lax
from jax.sharding import Mesh, PartitionSpec as P

N = 12288

coef_linear = 3.4445
coef_cubic = -4.775
coef_quintic = 2.0315

LO = ("x", "y_lo")
COL = ("y_hi", "core")
ROW = ("y_lo", "z", "x")
MESH = ("y_lo", "z", "x", "y_hi", "core")


def rest_of(x):
    return x - lax.reduce_precision(x, exponent_bits=8, mantissa_bits=7)


def dot_nt(a, b):
    return lax.dot_general(a, b, (((1,), (1,)), ((), ())), preferred_element_type=jnp.float32)


def swap_x_y_hi(block):
    pairs = [((x * 4 + y) * 2 + k, (y * 4 + x) * 2 + k) for x in range(4) for y in range(4) for k in range(2)]
    return lax.ppermute(block, ("x", "y_hi", "core"), pairs)


def spread(block, axis):
    return lax.all_to_all(jnp.broadcast_to(block[None], (8,) + block.shape), axis, 0, 0)


def sum_pieces(pieces, axis):
    me = lax.axis_index(axis)
    mine = jnp.arange(pieces.shape[0])[:, None, None] == me
    arrived = lax.all_to_all(jnp.where(mine, 0.0, pieces).astype(jnp.bfloat16), axis, 0, 0)
    own = lax.dynamic_slice(pieces, (me, 0, 0), (1,) + pieces.shape[1:], allow_negative_indices=False)[0]
    return own + arrived.astype(jnp.float32).sum(0)


def per_device(x_scaled):
    rows, cols = x_scaled.shape
    mine = jnp.arange(8)[:, None, None] == lax.axis_index("z")
    copies = jnp.where(mine, x_scaled, lax.reduce_precision(x_scaled, 8, 7)).astype(jnp.bfloat16)
    xb = copies[0]
    by_hi = lax.all_to_all(copies, "z", 0, 0).reshape(8 * rows, cols)
    pair = lax.all_gather(xb, "y_lo", axis=0)
    by_lo = [lax.all_gather(pair[y], "x", axis=0, tiled=True) for y in range(2)]

    tile = jnp.concatenate([dot_nt(part, by_hi) for part in by_lo]) * (1.0 / N)
    gram = sum_pieces(tile.reshape(8, rows, 8 * rows), ("core", "y_hi"))

    rounded = gram.astype(jnp.bfloat16)
    right = spread(rounded, "z").reshape(8 * rows, 8 * rows)
    right_other = lax.ppermute(right, "core", [(0, 1), (1, 0)])
    left = lax.all_gather(swap_x_y_hi(rounded), "y_lo", axis=0)
    left = lax.all_gather(left, "x", axis=0).reshape(4, 2, rows, 8 * rows)
    core = lax.axis_index("core")
    own = jnp.where(core == 0, left[:, 0], left[:, 1]).reshape(4 * rows, 8 * rows)
    other = jnp.where(core == 0, left[:, 1], left[:, 0]).reshape(4 * rows, 8 * rows)
    square = jnp.dot(own, right, preferred_element_type=jnp.float32) + jnp.dot(
        other, right_other, preferred_element_type=jnp.float32
    )
    square = sum_pieces(square.reshape(4, rows, 8 * rows), "y_hi")

    place = (lax.axis_index("y_hi"), core, 0, 0)
    at_home = lax.dynamic_slice(left, place, (1, 1, rows, 8 * rows), allow_negative_indices=False)[0, 0]
    column = lax.broadcasted_iota(jnp.int32, at_home.shape, 1) - lax.axis_index("z") * rows
    on_diagonal = column == lax.broadcasted_iota(jnp.int32, at_home.shape, 0)
    diagonal = jnp.where(on_diagonal, at_home.astype(jnp.float32), 0.0).sum(1, keepdims=True)
    square = square + rest_of(gram) * (2.0 * diagonal)

    poly = (coef_cubic * gram + coef_quintic * square).astype(jnp.bfloat16)
    poly = lax.all_gather(poly, COL, axis=0, tiled=True)
    product = jnp.dot(poly, by_hi, preferred_element_type=jnp.float32)
    return coef_linear * x_scaled + sum_pieces(product.reshape(8, rows, cols), LO)


def solution(mesh):
    fine = Mesh(mesh.devices.reshape(2, 8, 4, 4, 2), MESH)
    return jax.shard_map(
        per_device,
        mesh=fine,
        in_specs=(P(ROW, COL),),
        out_specs=P(ROW, COL),
        check_vma=False,
    )
```

```python
import jax
import jax.numpy as jnp
from jax import lax
from jax.sharding import Mesh, PartitionSpec as P

N = 12288

coef_linear = 3.4445
coef_cubic = -4.775
coef_quintic = 2.0315

LO = ("x", "y_lo")
COL = ("y_hi", "core")
ROW = ("y_lo", "z", "x")
MESH = ("y_lo", "z", "x", "y_hi", "core")


def rest_of(x):
    return x - lax.reduce_precision(x, exponent_bits=8, mantissa_bits=7)


def dot_nt(a, b):
    return lax.dot_general(a, b, (((1,), (1,)), ((), ())), preferred_element_type=jnp.float32)


def swap_x_y_hi(block):
    pairs = [((x * 4 + y) * 2 + k, (y * 4 + x) * 2 + k) for x in range(4) for y in range(4) for k in range(2)]
    return lax.ppermute(block, ("x", "y_hi", "core"), pairs)


def spread(block, axis):
    return lax.all_to_all(jnp.broadcast_to(block[None], (8,) + block.shape), axis, 0, 0)


def sum_pieces(pieces, axis):
    me = lax.axis_index(axis)
    mine = jnp.arange(pieces.shape[0])[:, None, None] == me
    arrived = lax.all_to_all(jnp.where(mine, 0.0, pieces).astype(jnp.bfloat16), axis, 0, 0)
    own = lax.dynamic_slice(pieces, (me, 0, 0), (1,) + pieces.shape[1:], allow_negative_indices=False)[0]
    return own + arrived.astype(jnp.float32).sum(0)


def per_device(x_scaled):
    rows, cols = x_scaled.shape
    xb = x_scaled.astype(jnp.bfloat16)
    by_hi = spread(xb, "z").reshape(8 * rows, cols)
    pair = lax.all_gather(xb, "y_lo", axis=0)
    by_lo = [lax.all_gather(pair[y], "x", axis=0, tiled=True) for y in range(2)]

    tile = jnp.concatenate([dot_nt(part, by_hi) for part in by_lo]) * (1.0 / N)
    gram = sum_pieces(tile.reshape(8, rows, 8 * rows), ("core", "y_hi"))

    rounded = gram.astype(jnp.bfloat16)
    right = spread(rounded, "z").reshape(8 * rows, 8 * rows)
    right_other = lax.ppermute(right, "core", [(0, 1), (1, 0)])
    left = lax.all_gather(swap_x_y_hi(rounded), "y_lo", axis=0)
    left = lax.all_gather(left, "x", axis=0).reshape(4, 2, rows, 8 * rows)
    core = lax.axis_index("core")
    own = jnp.where(core == 0, left[:, 0], left[:, 1]).reshape(4 * rows, 8 * rows)
    other = jnp.where(core == 0, left[:, 1], left[:, 0]).reshape(4 * rows, 8 * rows)
    square = jnp.dot(own, right, preferred_element_type=jnp.float32) + jnp.dot(
        other, right_other, preferred_element_type=jnp.float32
    )
    square = sum_pieces(square.reshape(4, rows, 8 * rows), "y_hi")

    place = (lax.axis_index("y_hi"), core, 0, 0)
    at_home = lax.dynamic_slice(left, place, (1, 1, rows, 8 * rows), allow_negative_indices=False)[0, 0]
    column = lax.broadcasted_iota(jnp.int32, at_home.shape, 1) - lax.axis_index("z") * rows
    on_diagonal = column == lax.broadcasted_iota(jnp.int32, at_home.shape, 0)
    diagonal = jnp.where(on_diagonal, at_home.astype(jnp.float32), 0.0).sum(1, keepdims=True)
    square = square + rest_of(gram) * (2.0 * diagonal)

    poly = (coef_cubic * gram + coef_quintic * square).astype(jnp.bfloat16)
    poly = lax.all_gather(poly, COL, axis=0, tiled=True)
    product = jnp.dot(poly, by_hi, preferred_element_type=jnp.float32)
    mine = jnp.arange(8)[:, None, None] == lax.axis_index(LO)
    linear = jnp.where(mine, coef_linear * x_scaled, 0.0)
    return sum_pieces(product.reshape(8, rows, cols) + linear, LO)


def solution(mesh):
    fine = Mesh(mesh.devices.reshape(2, 8, 4, 4, 2), MESH)
    return jax.shard_map(
        per_device,
        mesh=fine,
        in_specs=(P(ROW, COL),),
        out_specs=P(ROW, COL),
        check_vma=False,
    )
```

```python
import jax
import jax.numpy as jnp
from jax import lax
from jax.sharding import Mesh, PartitionSpec as P

N = 12288

coef_linear = 3.4445
coef_cubic = -4.775
coef_quintic = 2.0315

LO = ("x", "y_lo")
COL = ("y_hi", "core")
ROW = ("y_lo", "z", "x")
MESH = ("y_lo", "z", "x", "y_hi", "core")


def rest_of(x):
    return x - lax.reduce_precision(x, exponent_bits=8, mantissa_bits=7)


def dot_nt(a, b):
    return lax.dot_general(a, b, (((1,), (1,)), ((), ())), preferred_element_type=jnp.float32)


def swap_x_y_hi(block):
    pairs = [((x * 4 + y) * 2 + k, (y * 4 + x) * 2 + k) for x in range(4) for y in range(4) for k in range(2)]
    return lax.ppermute(block, ("x", "y_hi", "core"), pairs)


def spread(block, axis):
    return lax.all_to_all(jnp.broadcast_to(block[None], (8,) + block.shape), axis, 0, 0)


def sum_pieces(pieces, axis):
    me = lax.axis_index(axis)
    mine = jnp.arange(pieces.shape[0])[:, None, None] == me
    arrived = lax.all_to_all(jnp.where(mine, 0.0, pieces).astype(jnp.bfloat16), axis, 0, 0)
    own = lax.dynamic_slice(pieces, (me, 0, 0), (1,) + pieces.shape[1:], allow_negative_indices=False)[0]
    return own + arrived.astype(jnp.float32).sum(0)


def per_device(x_scaled):
    rows, cols = x_scaled.shape
    xb = x_scaled.astype(jnp.bfloat16)
    by_hi = spread(xb, "z").reshape(8 * rows, cols)
    pair = lax.all_gather(xb, "y_lo", axis=0)
    by_lo = [lax.all_gather(pair[y], "x", axis=0, tiled=True) for y in range(2)]

    tile = jnp.concatenate([dot_nt(part, by_hi) for part in by_lo]) * (1.0 / N)
    gram = sum_pieces(tile.reshape(8, rows, 8 * rows), ("core", "y_hi"))

    rounded = gram.astype(jnp.bfloat16)
    right = spread(rounded, "z").reshape(8 * rows, 8 * rows)
    right_other = lax.ppermute(right, "core", [(0, 1), (1, 0)])
    left = lax.all_gather(swap_x_y_hi(rounded), "y_lo", axis=0)
    left = lax.all_gather(left, "x", axis=0).reshape(4, 2, rows, 8 * rows)
    core = lax.axis_index("core")
    own = jnp.where(core == 0, left[:, 0], left[:, 1]).reshape(4 * rows, 8 * rows)
    other = jnp.where(core == 0, left[:, 1], left[:, 0]).reshape(4 * rows, 8 * rows)
    square = jnp.dot(own, right, preferred_element_type=jnp.float32) + jnp.dot(
        other, right_other, preferred_element_type=jnp.float32
    )
    square = sum_pieces(square.reshape(4, rows, 8 * rows), "y_hi")

    place = (lax.axis_index("y_hi"), core, 0, 0)
    at_home = lax.dynamic_slice(left, place, (1, 1, rows, 8 * rows), allow_negative_indices=False)[0, 0]
    column = lax.broadcasted_iota(jnp.int32, at_home.shape, 1) - lax.axis_index("z") * rows
    on_diagonal = column == lax.broadcasted_iota(jnp.int32, at_home.shape, 0)
    diagonal = jnp.where(on_diagonal, at_home.astype(jnp.float32), 0.0).sum(1, keepdims=True)
    square = square + rest_of(gram) * (2.0 * diagonal)

    poly = (coef_cubic * gram + coef_quintic * square).astype(jnp.bfloat16)
    poly = lax.all_gather(poly, COL, axis=0, tiled=True)
    product = jnp.dot(poly, by_hi, preferred_element_type=jnp.float32)
    mine = jnp.arange(8)[:, None, None] == lax.axis_index(LO)
    linear = coef_linear * jnp.where(mine, x_scaled, 0.0)
    return sum_pieces(product.reshape(8, rows, cols) + linear, LO)


def solution(mesh):
    fine = Mesh(mesh.devices.reshape(2, 8, 4, 4, 2), MESH)
    return jax.shard_map(
        per_device,
        mesh=fine,
        in_specs=(P(ROW, COL),),
        out_specs=P(ROW, COL),
        check_vma=False,
    )
```

```python
import jax
import jax.numpy as jnp
from jax import lax
from jax.sharding import Mesh, PartitionSpec as P

N = 12288

coef_linear = 3.4445
coef_cubic = -4.775
coef_quintic = 2.0315

LO = ("x", "y_lo")
COL = ("y_hi", "core")
ROW = ("y_lo", "z", "x")
MESH = ("y_lo", "z", "x", "y_hi", "core")


def rest_of(x):
    return x - lax.reduce_precision(x, exponent_bits=8, mantissa_bits=7)


def dot_nt(a, b):
    return lax.dot_general(a, b, (((1,), (1,)), ((), ())), preferred_element_type=jnp.float32)


def swap_x_y_hi(block):
    pairs = [((x * 4 + y) * 2 + k, (y * 4 + x) * 2 + k) for x in range(4) for y in range(4) for k in range(2)]
    return lax.ppermute(block, ("x", "y_hi", "core"), pairs)


def spread(block, axis):
    return lax.all_to_all(jnp.broadcast_to(block[None], (8,) + block.shape), axis, 0, 0)


def sum_pieces(pieces, axis):
    me = lax.axis_index(axis)
    mine = jnp.arange(pieces.shape[0])[:, None, None] == me
    arrived = lax.all_to_all(jnp.where(mine, 0.0, pieces).astype(jnp.bfloat16), axis, 0, 0)
    own = lax.dynamic_slice(pieces, (me, 0, 0), (1,) + pieces.shape[1:], allow_negative_indices=False)[0]
    return own + arrived.astype(jnp.float32).sum(0)


def per_device(x_scaled):
    rows, cols = x_scaled.shape
    copies = lax.optimization_barrier(jnp.broadcast_to(x_scaled.astype(jnp.bfloat16)[None], (8, rows, cols)))
    xb = copies[0]
    by_hi = lax.all_to_all(copies, "z", 0, 0).reshape(8 * rows, cols)
    pair = lax.all_gather(xb, "y_lo", axis=0)
    by_lo = [lax.all_gather(pair[y], "x", axis=0, tiled=True) for y in range(2)]

    tile = jnp.concatenate([dot_nt(part, by_hi) for part in by_lo]) * (1.0 / N)
    gram = sum_pieces(tile.reshape(8, rows, 8 * rows), ("core", "y_hi"))

    rounded = gram.astype(jnp.bfloat16)
    right = spread(rounded, "z").reshape(8 * rows, 8 * rows)
    right_other = lax.ppermute(right, "core", [(0, 1), (1, 0)])
    left = lax.all_gather(swap_x_y_hi(rounded), "y_lo", axis=0)
    left = lax.all_gather(left, "x", axis=0).reshape(4, 2, rows, 8 * rows)
    core = lax.axis_index("core")
    own = jnp.where(core == 0, left[:, 0], left[:, 1]).reshape(4 * rows, 8 * rows)
    other = jnp.where(core == 0, left[:, 1], left[:, 0]).reshape(4 * rows, 8 * rows)
    square = jnp.dot(own, right, preferred_element_type=jnp.float32) + jnp.dot(
        other, right_other, preferred_element_type=jnp.float32
    )
    square = sum_pieces(square.reshape(4, rows, 8 * rows), "y_hi")

    place = (lax.axis_index("y_hi"), core, 0, 0)
    at_home = lax.dynamic_slice(left, place, (1, 1, rows, 8 * rows), allow_negative_indices=False)[0, 0]
    column = lax.broadcasted_iota(jnp.int32, at_home.shape, 1) - lax.axis_index("z") * rows
    on_diagonal = column == lax.broadcasted_iota(jnp.int32, at_home.shape, 0)
    diagonal = jnp.where(on_diagonal, at_home.astype(jnp.float32), 0.0).sum(1, keepdims=True)
    square = square + rest_of(gram) * (2.0 * diagonal)

    poly = (coef_cubic * gram + coef_quintic * square).astype(jnp.bfloat16)
    poly = lax.all_gather(poly, COL, axis=0, tiled=True)
    product = jnp.dot(poly, by_hi, preferred_element_type=jnp.float32)
    mine = jnp.arange(8)[:, None, None] == lax.axis_index(LO)
    linear = coef_linear * jnp.where(mine, x_scaled, 0.0)
    return sum_pieces(product.reshape(8, rows, cols) + linear, LO)


def solution(mesh):
    fine = Mesh(mesh.devices.reshape(2, 8, 4, 4, 2), MESH)
    return jax.shard_map(
        per_device,
        mesh=fine,
        in_specs=(P(ROW, COL),),
        out_specs=P(ROW, COL),
        check_vma=False,
    )
```

```python
import jax
import jax.numpy as jnp
from jax import lax
from jax.sharding import Mesh, PartitionSpec as P

N = 12288

coef_linear = 3.4445
coef_cubic = -4.775
coef_quintic = 2.0315

LO = ("x", "y_lo")
COL = ("y_hi", "core")
ROW = ("y_lo", "z", "x")
MESH = ("y_lo", "z", "x", "y_hi", "core")


def rest_of(x):
    return x - lax.reduce_precision(x, exponent_bits=8, mantissa_bits=7)


def dot_nt(a, b):
    return lax.dot_general(a, b, (((1,), (1,)), ((), ())), preferred_element_type=jnp.float32)


def swap_x_y_hi(block):
    pairs = [((x * 4 + y) * 2 + k, (y * 4 + x) * 2 + k) for x in range(4) for y in range(4) for k in range(2)]
    return lax.ppermute(block, ("x", "y_hi", "core"), pairs)


def spread(block, axis):
    return lax.all_to_all(jnp.broadcast_to(block[None], (8,) + block.shape), axis, 0, 0)


def sum_pieces(pieces, axis, zero=0.0):
    me = lax.axis_index(axis)
    mine = jnp.arange(pieces.shape[0])[:, None, None] == me
    arrived = lax.all_to_all(jnp.where(mine, zero, pieces).astype(jnp.bfloat16), axis, 0, 0)
    own = lax.dynamic_slice(pieces, (me, 0, 0), (1,) + pieces.shape[1:], allow_negative_indices=False)[0]
    return own + arrived.astype(jnp.float32).sum(0)


def per_device(x_scaled):
    rows, cols = x_scaled.shape
    xb = x_scaled.astype(jnp.bfloat16)
    by_hi = spread(xb, "z").reshape(8 * rows, cols)
    pair = lax.all_gather(xb, "y_lo", axis=0)
    by_lo = [lax.all_gather(pair[y], "x", axis=0, tiled=True) for y in range(2)]

    tile = jnp.concatenate([dot_nt(part, by_hi) for part in by_lo]) * (1.0 / N)
    gram = sum_pieces(tile.reshape(8, rows, 8 * rows), ("core", "y_hi"))

    rounded = gram.astype(jnp.bfloat16)
    right = spread(rounded, "z").reshape(8 * rows, 8 * rows)
    right_other = lax.ppermute(right, "core", [(0, 1), (1, 0)])
    left = lax.all_gather(swap_x_y_hi(rounded), "y_lo", axis=0)
    left = lax.all_gather(left, "x", axis=0).reshape(4, 2, rows, 8 * rows)
    core = lax.axis_index("core")
    own = jnp.where(core == 0, left[:, 0], left[:, 1]).reshape(4 * rows, 8 * rows)
    other = jnp.where(core == 0, left[:, 1], left[:, 0]).reshape(4 * rows, 8 * rows)
    square = jnp.dot(own, right, preferred_element_type=jnp.float32) + jnp.dot(
        other, right_other, preferred_element_type=jnp.float32
    )
    place = (lax.axis_index("y_hi") * rows, 0)
    at_home = lax.dynamic_slice(own, place, (rows, 8 * rows), allow_negative_indices=False)
    column = lax.broadcasted_iota(jnp.int32, at_home.shape, 1) - lax.axis_index("z") * rows
    on_diagonal = column == lax.broadcasted_iota(jnp.int32, at_home.shape, 0)
    diagonal = jnp.where(on_diagonal, at_home.astype(jnp.float32), 0.0).sum(1, keepdims=True)
    square = sum_pieces(square.reshape(4, rows, 8 * rows), "y_hi", 0.0 * diagonal[0, 0])
    square = square + rest_of(gram) * (2.0 * diagonal)

    poly = (coef_cubic * gram + coef_quintic * square).astype(jnp.bfloat16)
    poly = lax.all_gather(poly, COL, axis=0, tiled=True)
    product = jnp.dot(poly, by_hi, preferred_element_type=jnp.float32)
    mine = jnp.arange(8)[:, None, None] == lax.axis_index(LO)
    linear = coef_linear * jnp.where(mine, x_scaled, 0.0)
    return sum_pieces(product.reshape(8, rows, cols) + linear, LO)


def solution(mesh):
    fine = Mesh(mesh.devices.reshape(2, 8, 4, 4, 2), MESH)
    return jax.shard_map(
        per_device,
        mesh=fine,
        in_specs=(P(ROW, COL),),
        out_specs=P(ROW, COL),
        check_vma=False,
    )
```

```python
import jax
import jax.numpy as jnp
from jax import lax
from jax.sharding import Mesh, PartitionSpec as P

N = 12288

coef_linear = 3.4445
coef_cubic = -4.775
coef_quintic = 2.0315

LO = ("x", "y_lo")
COL = ("y_hi", "core")
HI = ("z_hi", "z_lo")
ROW = ("y_lo",) + HI + ("x",)
MESH = ("y_lo", "z_hi", "z_lo", "x", "y_hi", "core")


def rest_of(x):
    return x - lax.reduce_precision(x, exponent_bits=8, mantissa_bits=7)


def dot_nt(a, b):
    return lax.dot_general(a, b, (((1,), (1,)), ((), ())), preferred_element_type=jnp.float32)


def swap_x_y_hi(block):
    pairs = [((x * 4 + y) * 2 + k, (y * 4 + x) * 2 + k) for x in range(4) for y in range(4) for k in range(2)]
    return lax.ppermute(block, ("x", "y_hi", "core"), pairs)


def spread(block, axis):
    return lax.all_to_all(jnp.broadcast_to(block[None], (8,) + block.shape), axis, 0, 0)


def sum_pieces(pieces, axis):
    me = lax.axis_index(axis)
    mine = jnp.arange(pieces.shape[0])[:, None, None] == me
    arrived = lax.all_to_all(jnp.where(mine, 0.0, pieces).astype(jnp.bfloat16), axis, 0, 0)
    own = lax.dynamic_slice(pieces, (me, 0, 0), (1,) + pieces.shape[1:], allow_negative_indices=False)[0]
    return own + arrived.astype(jnp.float32).sum(0)


def per_device(x_scaled):
    rows, cols = x_scaled.shape
    xb = x_scaled.astype(jnp.bfloat16)
    by_hi = spread(xb, HI).reshape(8 * rows, cols)
    pair = lax.all_gather(xb, "y_lo", axis=0)
    by_lo = [lax.all_gather(pair[y], "x", axis=0, tiled=True) for y in range(2)]

    tile = jnp.concatenate([dot_nt(part, by_hi) for part in by_lo]) * (1.0 / N)
    gram = sum_pieces(tile.reshape(8, rows, 8 * rows), ("core", "y_hi"))

    rounded = gram.astype(jnp.bfloat16)
    left = spread(swap_x_y_hi(rounded), LO).reshape(4, 2, rows, 8 * rows)
    right = lax.all_gather(rounded, "z_lo", axis=0, tiled=True)
    right = lax.all_gather(right, "z_hi", axis=0, tiled=True)
    right_other = lax.ppermute(right, "core", [(0, 1), (1, 0)])
    core = lax.axis_index("core")
    own = jnp.where(core == 0, left[:, 0], left[:, 1]).reshape(4 * rows, 8 * rows)
    other = jnp.where(core == 0, left[:, 1], left[:, 0]).reshape(4 * rows, 8 * rows)
    square = jnp.dot(own, right, preferred_element_type=jnp.float32) + jnp.dot(
        other, right_other, preferred_element_type=jnp.float32
    )
    square = sum_pieces(square.reshape(4, rows, 8 * rows), "y_hi")

    place = (lax.axis_index("y_hi"), core, 0, 0)
    at_home = lax.dynamic_slice(left, place, (1, 1, rows, 8 * rows), allow_negative_indices=False)[0, 0]
    column = lax.broadcasted_iota(jnp.int32, at_home.shape, 1) - lax.axis_index(HI) * rows
    on_diagonal = column == lax.broadcasted_iota(jnp.int32, at_home.shape, 0)
    diagonal = jnp.where(on_diagonal, at_home.astype(jnp.float32), 0.0).sum(1, keepdims=True)
    square = square + rest_of(gram) * (2.0 * diagonal)

    poly = (coef_cubic * gram + coef_quintic * square).astype(jnp.bfloat16)
    poly = lax.all_gather(poly, COL, axis=0, tiled=True)
    product = jnp.dot(poly, by_hi, preferred_element_type=jnp.float32)
    mine = jnp.arange(8)[:, None, None] == lax.axis_index(LO)
    linear = coef_linear * jnp.where(mine, x_scaled, 0.0)
    return sum_pieces(product.reshape(8, rows, cols) + linear, LO)


def solution(mesh):
    fine = Mesh(mesh.devices.reshape(2, 4, 2, 4, 4, 2), MESH)
    return jax.shard_map(
        per_device,
        mesh=fine,
        in_specs=(P(ROW, COL),),
        out_specs=P(ROW, COL),
        check_vma=False,
    )
```

```python
import jax
import jax.numpy as jnp
from jax import lax
from jax.sharding import Mesh, PartitionSpec as P

N = 12288

coef_linear = 3.4445
coef_cubic = -4.775
coef_quintic = 2.0315

LO = ("x", "y_lo")
COL = ("y_hi", "core")
ROW = ("y_lo", "z", "x")
MESH = ("y_lo", "z", "x", "y_hi", "core")


def rest_of(x):
    return x - lax.reduce_precision(x, exponent_bits=8, mantissa_bits=7)


def dot_nt(a, b):
    return lax.dot_general(a, b, (((1,), (1,)), ((), ())), preferred_element_type=jnp.float32)


def swap_x_y_hi(block):
    pairs = [((x * 4 + y) * 2 + k, (y * 4 + x) * 2 + k) for x in range(4) for y in range(4) for k in range(2)]
    return lax.ppermute(block, ("x", "y_hi", "core"), pairs)


def spread(block, axis):
    count = lax.axis_size(axis)
    return lax.all_to_all(jnp.broadcast_to(block[None], (count,) + block.shape), axis, 0, 0)


def sum_pieces(pieces, axis):
    me = lax.axis_index(axis)
    mine = jnp.arange(pieces.shape[0])[:, None, None] == me
    arrived = lax.all_to_all(jnp.where(mine, 0.0, pieces).astype(jnp.bfloat16), axis, 0, 0)
    own = lax.dynamic_slice(pieces, (me, 0, 0), (1,) + pieces.shape[1:], allow_negative_indices=False)[0]
    return own + arrived.astype(jnp.float32).sum(0)


def per_device(x_scaled):
    rows, cols = x_scaled.shape
    xb = x_scaled.astype(jnp.bfloat16)
    by_hi = spread(xb, "z").reshape(8 * rows, cols)
    pair = lax.all_gather(xb, "y_lo", axis=0)
    by_lo = [lax.all_gather(pair[y], "x", axis=0, tiled=True) for y in range(2)]

    tile = jnp.concatenate([dot_nt(part, by_hi) for part in by_lo]) * (1.0 / N)
    gram = sum_pieces(tile.reshape(8, rows, 8 * rows), ("core", "y_hi"))

    rounded = gram.astype(jnp.bfloat16)
    right = spread(rounded, "z").reshape(8 * rows, 8 * rows)
    right_other = lax.ppermute(right, "core", [(0, 1), (1, 0)])
    left = lax.all_gather(swap_x_y_hi(rounded), "y_lo", axis=0)
    left = spread(left + 0 * right_other[:1, :1], "x")
    core = lax.axis_index("core")
    own = jnp.where(core == 0, left[:, 0], left[:, 1]).reshape(4 * rows, 8 * rows)
    other = jnp.where(core == 0, left[:, 1], left[:, 0]).reshape(4 * rows, 8 * rows)
    square = jnp.dot(own, right, preferred_element_type=jnp.float32) + jnp.dot(
        other, right_other, preferred_element_type=jnp.float32
    )
    square = sum_pieces(square.reshape(4, rows, 8 * rows), "y_hi")

    place = (lax.axis_index("y_hi"), core, 0, 0)
    at_home = lax.dynamic_slice(left, place, (1, 1, rows, 8 * rows), allow_negative_indices=False)[0, 0]
    column = lax.broadcasted_iota(jnp.int32, at_home.shape, 1) - lax.axis_index("z") * rows
    on_diagonal = column == lax.broadcasted_iota(jnp.int32, at_home.shape, 0)
    diagonal = jnp.where(on_diagonal, at_home.astype(jnp.float32), 0.0).sum(1, keepdims=True)
    square = square + rest_of(gram) * (2.0 * diagonal)

    poly = (coef_cubic * gram + coef_quintic * square).astype(jnp.bfloat16)
    poly = lax.all_gather(poly, COL, axis=0, tiled=True)
    product = jnp.dot(poly, by_hi, preferred_element_type=jnp.float32)
    mine = jnp.arange(8)[:, None, None] == lax.axis_index(LO)
    linear = coef_linear * jnp.where(mine, x_scaled, 0.0)
    return sum_pieces(product.reshape(8, rows, cols) + linear, LO)


def solution(mesh):
    fine = Mesh(mesh.devices.reshape(2, 8, 4, 4, 2), MESH)
    return jax.shard_map(
        per_device,
        mesh=fine,
        in_specs=(P(ROW, COL),),
        out_specs=P(ROW, COL),
        check_vma=False,
    )
```

```python
import jax
import jax.numpy as jnp
from jax import lax
from jax.sharding import Mesh, PartitionSpec as P

N = 12288

coef_linear = 3.4445
coef_cubic = -4.775
coef_quintic = 2.0315

LO = ("x", "y_lo")
COL = ("y_hi", "core")
ROW = ("y_lo", "z", "x")
MESH = ("y_lo", "z", "x", "y_hi", "core")


def rest_of(x):
    return x - lax.reduce_precision(x, exponent_bits=8, mantissa_bits=7)


def dot_nt(a, b):
    return lax.dot_general(a, b, (((1,), (1,)), ((), ())), preferred_element_type=jnp.float32)


def swap_x_y_hi(block):
    pairs = [((x * 4 + y) * 2 + k, (y * 4 + x) * 2 + k) for x in range(4) for y in range(4) for k in range(2)]
    return lax.ppermute(block, ("x", "y_hi", "core"), pairs)


def spread(block, axis):
    return lax.all_to_all(jnp.broadcast_to(block[None], (8,) + block.shape), axis, 0, 0)


def sum_pieces(pieces, axis):
    me = lax.axis_index(axis)
    mine = jnp.arange(pieces.shape[0])[:, None, None] == me
    arrived = lax.all_to_all(jnp.where(mine, 0.0, pieces).astype(jnp.bfloat16), axis, 0, 0)
    own = lax.dynamic_slice(pieces, (me, 0, 0), (1,) + pieces.shape[1:], allow_negative_indices=False)[0]
    return own + arrived.astype(jnp.float32).sum(0)


def per_device(x_scaled):
    rows, cols = x_scaled.shape
    xb = x_scaled.astype(jnp.bfloat16)
    by_hi = spread(xb, "z").reshape(8 * rows, cols)
    pair = lax.all_gather(xb, "y_lo", axis=0)
    by_lo = [lax.all_gather(pair[y], "x", axis=0, tiled=True) for y in range(2)]

    core = lax.axis_index("core")
    tiles = [dot_nt(part, by_hi) * (1.0 / N) for part in by_lo]
    away = lax.ppermute(jnp.where(core == 0, tiles[1], tiles[0]), "core", [(0, 1), (1, 0)])
    home = jnp.where(core == 0, tiles[0], tiles[1]) + away
    gram = sum_pieces(home.reshape(4, rows, 8 * rows), "y_hi")

    rounded = gram.astype(jnp.bfloat16)
    right = spread(rounded, "z").reshape(8 * rows, 8 * rows)
    right_other = lax.ppermute(right, "core", [(0, 1), (1, 0)])
    left = lax.all_gather(swap_x_y_hi(rounded), "y_lo", axis=0)
    left = lax.all_gather(left, "x", axis=0).reshape(4, 2, rows, 8 * rows)
    own = jnp.where(core == 0, left[:, 0], left[:, 1]).reshape(4 * rows, 8 * rows)
    other = jnp.where(core == 0, left[:, 1], left[:, 0]).reshape(4 * rows, 8 * rows)
    square = jnp.dot(own, right, preferred_element_type=jnp.float32) + jnp.dot(
        other, right_other, preferred_element_type=jnp.float32
    )
    square = sum_pieces(square.reshape(4, rows, 8 * rows), "y_hi")

    place = (lax.axis_index("y_hi"), core, 0, 0)
    at_home = lax.dynamic_slice(left, place, (1, 1, rows, 8 * rows), allow_negative_indices=False)[0, 0]
    column = lax.broadcasted_iota(jnp.int32, at_home.shape, 1) - lax.axis_index("z") * rows
    on_diagonal = column == lax.broadcasted_iota(jnp.int32, at_home.shape, 0)
    diagonal = jnp.where(on_diagonal, at_home.astype(jnp.float32), 0.0).sum(1, keepdims=True)
    square = square + rest_of(gram) * (2.0 * diagonal)

    poly = (coef_cubic * gram + coef_quintic * square).astype(jnp.bfloat16)
    poly = lax.all_gather(poly, COL, axis=0, tiled=True)
    product = jnp.dot(poly, by_hi, preferred_element_type=jnp.float32)
    mine = jnp.arange(8)[:, None, None] == lax.axis_index(LO)
    linear = coef_linear * jnp.where(mine, x_scaled, 0.0)
    return sum_pieces(product.reshape(8, rows, cols) + linear, LO)


def solution(mesh):
    fine = Mesh(mesh.devices.reshape(2, 8, 4, 4, 2), MESH)
    return jax.shard_map(
        per_device,
        mesh=fine,
        in_specs=(P(ROW, COL),),
        out_specs=P(ROW, COL),
        check_vma=False,
    )
```

```python
import jax
import jax.numpy as jnp
from jax import lax
from jax.sharding import Mesh, PartitionSpec as P

N = 12288

coef_linear = 3.4445
coef_cubic = -4.775
coef_quintic = 2.0315

LO = ("x", "y_lo")
Y_HI = ("y_hh", "y_hl")
COL = Y_HI + ("core",)
ROW = ("y_lo", "z", "x")
MESH = ("y_lo", "z", "x") + COL


def rest_of(x):
    return x - lax.reduce_precision(x, exponent_bits=8, mantissa_bits=7)


def dot_nt(a, b):
    return lax.dot_general(a, b, (((1,), (1,)), ((), ())), preferred_element_type=jnp.float32)


def swap_x_y_hi(block):
    pairs = [((x * 4 + y) * 2 + k, (y * 4 + x) * 2 + k) for x in range(4) for y in range(4) for k in range(2)]
    return lax.ppermute(block, ("x",) + COL, pairs)


def spread(block, axis):
    return lax.all_to_all(jnp.broadcast_to(block[None], (8,) + block.shape), axis, 0, 0)


def sum_pieces(pieces, axis):
    me = lax.axis_index(axis)
    mine = jnp.arange(pieces.shape[0])[:, None, None] == me
    arrived = lax.all_to_all(jnp.where(mine, 0.0, pieces).astype(jnp.bfloat16), axis, 0, 0)
    own = lax.dynamic_slice(pieces, (me, 0, 0), (1,) + pieces.shape[1:], allow_negative_indices=False)[0]
    return own + arrived.astype(jnp.float32).sum(0)


def per_device(x_scaled):
    rows, cols = x_scaled.shape
    xb = x_scaled.astype(jnp.bfloat16)
    by_hi = spread(xb, "z").reshape(8 * rows, cols)
    four = lax.all_gather(xb, "x", axis=0, tiled=True)
    by_lo = [lax.all_gather(half, "y_lo", axis=0, tiled=True) for half in (four[: 2 * rows], four[2 * rows :])]

    tile = jnp.concatenate([dot_nt(part, by_hi) for part in by_lo]) * (1.0 / N)
    gram = sum_pieces(tile.reshape(8, rows, 8 * rows), ("y_hh", "core", "y_hl"))

    rounded = gram.astype(jnp.bfloat16)
    right = spread(rounded, "z").reshape(8 * rows, 8 * rows)
    right_other = lax.ppermute(right, "core", [(0, 1), (1, 0)])
    left = lax.all_gather(swap_x_y_hi(rounded), "y_lo", axis=0)
    left = lax.all_gather(left, "x", axis=0).reshape(4, 2, rows, 8 * rows)
    core = lax.axis_index("core")
    own = jnp.where(core == 0, left[:, 0], left[:, 1]).reshape(4 * rows, 8 * rows)
    other = jnp.where(core == 0, left[:, 1], left[:, 0]).reshape(4 * rows, 8 * rows)
    square = jnp.dot(own, right, preferred_element_type=jnp.float32) + jnp.dot(
        other, right_other, preferred_element_type=jnp.float32
    )
    square = sum_pieces(square.reshape(4, rows, 8 * rows), Y_HI)

    place = (lax.axis_index(Y_HI), core, 0, 0)
    at_home = lax.dynamic_slice(left, place, (1, 1, rows, 8 * rows), allow_negative_indices=False)[0, 0]
    column = lax.broadcasted_iota(jnp.int32, at_home.shape, 1) - lax.axis_index("z") * rows
    on_diagonal = column == lax.broadcasted_iota(jnp.int32, at_home.shape, 0)
    diagonal = jnp.where(on_diagonal, at_home.astype(jnp.float32), 0.0).sum(1, keepdims=True)
    square = square + rest_of(gram) * (2.0 * diagonal)

    poly = (coef_cubic * gram + coef_quintic * square).astype(jnp.bfloat16)
    poly = lax.all_gather(poly, COL, axis=0, tiled=True)
    product = jnp.dot(poly, by_hi, preferred_element_type=jnp.float32)
    mine = jnp.arange(8)[:, None, None] == lax.axis_index(LO)
    linear = coef_linear * jnp.where(mine, x_scaled, 0.0)
    return sum_pieces(product.reshape(8, rows, cols) + linear, LO)


def solution(mesh):
    fine = Mesh(mesh.devices.reshape(2, 8, 4, 2, 2, 2), MESH)
    return jax.shard_map(
        per_device,
        mesh=fine,
        in_specs=(P(ROW, COL),),
        out_specs=P(ROW, COL),
        check_vma=False,
    )
```

```python
import jax
import jax.numpy as jnp
from jax import lax
from jax.sharding import Mesh, PartitionSpec as P

N = 12288

coef_linear = 3.4445
coef_cubic = -4.775
coef_quintic = 2.0315

LO = ("x", "y_lo")
Y_HI = ("y_hh", "y_hl")
COL = Y_HI + ("core",)
ROW = ("y_lo", "z", "x")
MESH = ("y_lo", "z", "x") + COL


def rest_of(x):
    return x - lax.reduce_precision(x, exponent_bits=8, mantissa_bits=7)


def dot_nt(a, b):
    return lax.dot_general(a, b, (((1,), (1,)), ((), ())), preferred_element_type=jnp.float32)


def swap_x_y_hi(block):
    pairs = [((x * 4 + y) * 2 + k, (y * 4 + x) * 2 + k) for x in range(4) for y in range(4) for k in range(2)]
    return lax.ppermute(block, ("x",) + COL, pairs)


def spread(block, axis):
    return lax.all_to_all(jnp.broadcast_to(block[None], (8,) + block.shape), axis, 0, 0)


def sum_pieces(pieces, axis):
    me = lax.axis_index(axis)
    mine = jnp.arange(pieces.shape[0])[:, None, None] == me
    arrived = lax.all_to_all(jnp.where(mine, 0.0, pieces).astype(jnp.bfloat16), axis, 0, 0)
    own = lax.dynamic_slice(pieces, (me, 0, 0), (1,) + pieces.shape[1:], allow_negative_indices=False)[0]
    return own + arrived.astype(jnp.float32).sum(0)


def per_device(x_scaled):
    rows, cols = x_scaled.shape
    ones = 1.0 + 0.0 * (jnp.arange(8) * lax.axis_index("z")).astype(jnp.float32)
    copies = lax.optimization_barrier((x_scaled * ones[:, None, None]).astype(jnp.bfloat16))
    xb = copies[0]
    by_hi = lax.all_to_all(copies, "z", 0, 0).reshape(8 * rows, cols)
    four = lax.all_gather(xb, "x", axis=0, tiled=True)
    by_lo = [lax.all_gather(half, "y_lo", axis=0, tiled=True) for half in (four[: 2 * rows], four[2 * rows :])]

    tile = jnp.concatenate([dot_nt(part, by_hi).reshape(2, 2 * rows, 8 * rows) for part in by_lo], axis=1) * (1.0 / N)
    gram = sum_pieces(tile.reshape(8, rows, 8 * rows), ("core",) + Y_HI)

    rounded = gram.astype(jnp.bfloat16)
    right = spread(rounded, "z").reshape(8 * rows, 8 * rows)
    right_other = lax.ppermute(right, "core", [(0, 1), (1, 0)])
    left = lax.all_gather(swap_x_y_hi(rounded), "y_lo", axis=0)
    left = lax.all_gather(left, "x", axis=0).reshape(4, 2, rows, 8 * rows)
    core = lax.axis_index("core")
    own = jnp.where(core == 0, left[:, 0], left[:, 1]).reshape(4 * rows, 8 * rows)
    other = jnp.where(core == 0, left[:, 1], left[:, 0]).reshape(4 * rows, 8 * rows)
    square = jnp.dot(own, right, preferred_element_type=jnp.float32) + jnp.dot(
        other, right_other, preferred_element_type=jnp.float32
    )
    square = sum_pieces(square.reshape(4, rows, 8 * rows), Y_HI)

    place = (lax.axis_index(Y_HI), core, 0, 0)
    at_home = lax.dynamic_slice(left, place, (1, 1, rows, 8 * rows), allow_negative_indices=False)[0, 0]
    column = lax.broadcasted_iota(jnp.int32, at_home.shape, 1) - lax.axis_index("z") * rows
    on_diagonal = column == lax.broadcasted_iota(jnp.int32, at_home.shape, 0)
    diagonal = jnp.where(on_diagonal, at_home.astype(jnp.float32), 0.0).sum(1, keepdims=True)
    square = square + rest_of(gram) * (2.0 * diagonal)

    poly = (coef_cubic * gram + coef_quintic * square).astype(jnp.bfloat16)
    poly = lax.all_gather(poly, COL, axis=0, tiled=True)
    product = jnp.dot(poly, by_hi, preferred_element_type=jnp.float32)
    mine = jnp.arange(8)[:, None, None] == lax.axis_index(LO)
    linear = coef_linear * jnp.where(mine, x_scaled, 0.0)
    return sum_pieces(product.reshape(8, rows, cols) + linear, LO)


def solution(mesh):
    fine = Mesh(mesh.devices.reshape(2, 8, 4, 2, 2, 2), MESH)
    return jax.shard_map(
        per_device,
        mesh=fine,
        in_specs=(P(ROW, COL),),
        out_specs=P(ROW, COL),
        check_vma=False,
    )
```

```python
import jax
import jax.numpy as jnp
from jax import lax
from jax.sharding import Mesh, PartitionSpec as P

N = 12288

coef_linear = 3.4445
coef_cubic = -4.775
coef_quintic = 2.0315

LO = ("x", "y_lo")
Y_HI = ("y_hh", "y_hl")
COL = Y_HI + ("core",)
ROW = ("y_lo", "z", "x")
MESH = ("y_lo", "z", "x") + COL


def rest_of(x):
    return x - lax.reduce_precision(x, exponent_bits=8, mantissa_bits=7)


def dot_nt(a, b):
    return lax.dot_general(a, b, (((1,), (1,)), ((), ())), preferred_element_type=jnp.float32)


def swap_x_y_hi(block):
    pairs = [((x * 4 + y) * 2 + k, (y * 4 + x) * 2 + k) for x in range(4) for y in range(4) for k in range(2)]
    return lax.ppermute(block, ("x",) + COL, pairs)


def spread(block, axis):
    return lax.all_to_all(jnp.broadcast_to(block[None], (8,) + block.shape), axis, 0, 0)


def sum_pieces(pieces, axis):
    me = lax.axis_index(axis)
    mine = jnp.arange(pieces.shape[0])[:, None, None] == me
    arrived = lax.all_to_all(jnp.where(mine, 0.0, pieces).astype(jnp.bfloat16), axis, 0, 0)
    own = lax.dynamic_slice(pieces, (me, 0, 0), (1,) + pieces.shape[1:], allow_negative_indices=False)[0]
    return own + arrived.astype(jnp.float32).sum(0)


def per_device(x_scaled):
    rows, cols = x_scaled.shape
    xb = x_scaled.astype(jnp.bfloat16)
    by_hi = spread(xb, "z").reshape(8 * rows, cols)
    four = lax.all_gather(xb, "x", axis=0, tiled=True)
    by_lo = [lax.all_gather(half, "y_lo", axis=0, tiled=True) for half in (four[: 2 * rows], four[2 * rows :])]

    tile = jnp.concatenate([dot_nt(part, by_hi).reshape(2, 2 * rows, 8 * rows) for part in by_lo], axis=1) * (1.0 / N)
    gram = sum_pieces(tile.reshape(8, rows, 8 * rows), ("core",) + Y_HI)

    rounded = gram.astype(jnp.bfloat16)
    right = spread(rounded, "z").reshape(8 * rows, 8 * rows)
    right_other = lax.ppermute(right, "core", [(0, 1), (1, 0)])
    left = lax.all_gather(swap_x_y_hi(rounded), "y_lo", axis=0)
    left = lax.all_gather(left, "x", axis=0).reshape(4, 2, rows, 8 * rows)
    core = lax.axis_index("core")
    own = jnp.where(core == 0, left[:, 0], left[:, 1]).reshape(4 * rows, 8 * rows)
    other = jnp.where(core == 0, left[:, 1], left[:, 0]).reshape(4 * rows, 8 * rows)
    square = jnp.dot(own, right, preferred_element_type=jnp.float32) + jnp.dot(
        other, right_other, preferred_element_type=jnp.float32
    )
    square = sum_pieces(square.reshape(4, rows, 8 * rows), Y_HI)

    place = (lax.axis_index(Y_HI), core, 0, 0)
    at_home = lax.dynamic_slice(left, place, (1, 1, rows, 8 * rows), allow_negative_indices=False)[0, 0]
    column = lax.broadcasted_iota(jnp.int32, at_home.shape, 1) - lax.axis_index("z") * rows
    on_diagonal = column == lax.broadcasted_iota(jnp.int32, at_home.shape, 0)
    diagonal = jnp.where(on_diagonal, at_home.astype(jnp.float32), 0.0).sum(1, keepdims=True)
    square = square + rest_of(gram) * (2.0 * diagonal)

    poly = (coef_cubic * gram + coef_quintic * square).astype(jnp.bfloat16)
    poly = lax.all_gather(poly, COL, axis=0, tiled=True)
    product = jnp.dot(poly, by_hi, preferred_element_type=jnp.float32)
    mine = jnp.arange(8)[:, None, None] == lax.axis_index(LO)
    linear = coef_linear * jnp.where(mine, x_scaled, 0.0)
    return sum_pieces(product.reshape(8, rows, cols) + linear, LO)


def solution(mesh):
    fine = Mesh(mesh.devices.reshape(2, 8, 4, 2, 2, 2), MESH)
    return jax.shard_map(
        per_device,
        mesh=fine,
        in_specs=(P(ROW, COL),),
        out_specs=P(ROW, COL),
        check_vma=False,
    )
```

```python
import jax
import jax.numpy as jnp
from jax import lax
from jax.sharding import Mesh, PartitionSpec as P

N = 12288

coef_linear = 3.4445
coef_cubic = -4.775
coef_quintic = 2.0315

LO = ("x", "y_lo")
COL = ("y_hi", "core")
ROW = ("y_lo", "z", "x")
MESH = ("y_lo", "z", "x", "y_hi", "core")


def rest_of(x):
    return x - lax.reduce_precision(x, exponent_bits=8, mantissa_bits=7)


def dot_nt(a, b):
    return lax.dot_general(a, b, (((1,), (1,)), ((), ())), preferred_element_type=jnp.float32)


def swap_x_y_hi(block):
    pairs = [((x * 4 + y) * 2 + k, (y * 4 + x) * 2 + k) for x in range(4) for y in range(4) for k in range(2)]
    return lax.ppermute(block, ("x", "y_hi", "core"), pairs)


def spread(block, axis):
    return lax.all_to_all(jnp.broadcast_to(block[None], (8,) + block.shape), axis, 0, 0)


def sum_pieces(pieces, axis, zero=0.0):
    me = lax.axis_index(axis)
    mine = jnp.arange(pieces.shape[0])[:, None, None] == me
    arrived = lax.all_to_all(jnp.where(mine, zero, pieces).astype(jnp.bfloat16), axis, 0, 0)
    own = lax.dynamic_slice(pieces, (me, 0, 0), (1,) + pieces.shape[1:], allow_negative_indices=False)[0]
    return own + arrived.astype(jnp.float32).sum(0)


def per_device(x_scaled):
    rows, cols = x_scaled.shape
    xb = x_scaled.astype(jnp.bfloat16)
    by_hi = spread(xb, "z").reshape(8 * rows, cols)
    pair = lax.all_gather(xb, "y_lo", axis=0)
    by_lo = [lax.all_gather(pair[y], "x", axis=0, tiled=True) for y in range(2)]

    tile = jnp.concatenate([dot_nt(part, by_hi) for part in by_lo]) * (1.0 / N)
    gram = sum_pieces(tile.reshape(8, rows, 8 * rows), ("core", "y_hi"))

    rounded = gram.astype(jnp.bfloat16)
    right = spread(rounded, "z").reshape(8 * rows, 8 * rows)
    right_other = lax.ppermute(right, "core", [(0, 1), (1, 0)])
    left = lax.all_gather(swap_x_y_hi(rounded), "y_lo", axis=0)
    left = lax.all_gather(left, "x", axis=0).reshape(4, 2, rows, 8 * rows)
    core = lax.axis_index("core")
    own = jnp.where(core == 0, left[:, 0], left[:, 1]).reshape(4 * rows, 8 * rows)
    other = jnp.where(core == 0, left[:, 1], left[:, 0]).reshape(4 * rows, 8 * rows)
    square = jnp.dot(own, right, preferred_element_type=jnp.float32) + jnp.dot(
        other, right_other, preferred_element_type=jnp.float32
    )
    place = (lax.axis_index("y_hi"), core, 0, 0)
    at_home = lax.dynamic_slice(left, place, (1, 1, rows, 8 * rows), allow_negative_indices=False)[0, 0]
    column = lax.broadcasted_iota(jnp.int32, at_home.shape, 1) - lax.axis_index("z") * rows
    on_diagonal = column == lax.broadcasted_iota(jnp.int32, at_home.shape, 0)
    diagonal = jnp.where(on_diagonal, at_home.astype(jnp.float32), 0.0).sum(1, keepdims=True)
    twice = 2.0 * diagonal
    square = sum_pieces(square.reshape(4, rows, 8 * rows), "y_hi", 0.0 * twice[0, 0])
    square = square + rest_of(gram) * twice

    poly = (coef_cubic * gram + coef_quintic * square).astype(jnp.bfloat16)
    poly = lax.all_gather(poly, COL, axis=0, tiled=True)
    product = jnp.dot(poly, by_hi, preferred_element_type=jnp.float32)
    mine = jnp.arange(8)[:, None, None] == lax.axis_index(LO)
    linear = coef_linear * jnp.where(mine, x_scaled, 0.0)
    return sum_pieces(product.reshape(8, rows, cols) + linear, LO)


def solution(mesh):
    fine = Mesh(mesh.devices.reshape(2, 8, 4, 4, 2), MESH)
    return jax.shard_map(
        per_device,
        mesh=fine,
        in_specs=(P(ROW, COL),),
        out_specs=P(ROW, COL),
        check_vma=False,
    )
```

```python
import jax
import jax.numpy as jnp
from jax import lax
from jax.sharding import Mesh, PartitionSpec as P

N = 12288

coef_linear = 3.4445
coef_cubic = -4.775
coef_quintic = 2.0315

LO = ("x", "y_lo")
COL = ("y_hi", "core")
ROW = ("y_lo", "z", "x")
MESH = ("y_lo", "z", "x", "y_hi", "core")


def rest_of(x):
    return x - lax.reduce_precision(x, exponent_bits=8, mantissa_bits=7)


def dot_nt(a, b):
    return lax.dot_general(a, b, (((1,), (1,)), ((), ())), preferred_element_type=jnp.float32)


def swap_x_y_hi(block):
    pairs = [((x * 4 + y) * 2 + k, (y * 4 + x) * 2 + k) for x in range(4) for y in range(4) for k in range(2)]
    return lax.ppermute(block, ("x", "y_hi", "core"), pairs)


def spread(block, axis):
    count = lax.axis_size(axis)
    return lax.all_to_all(jnp.broadcast_to(block[None], (count,) + block.shape), axis, 0, 0)


def sum_pieces(pieces, axis):
    me = lax.axis_index(axis)
    mine = jnp.arange(pieces.shape[0])[:, None, None] == me
    arrived = lax.all_to_all(jnp.where(mine, 0.0, pieces).astype(jnp.bfloat16), axis, 0, 0)
    own = lax.dynamic_slice(pieces, (me, 0, 0), (1,) + pieces.shape[1:], allow_negative_indices=False)[0]
    return own + arrived.astype(jnp.float32).sum(0)


def per_device(x_scaled):
    rows, cols = x_scaled.shape
    xb = x_scaled.astype(jnp.bfloat16)
    by_hi = spread(xb, "z").reshape(8 * rows, cols)
    pair = lax.all_gather(xb, "y_lo", axis=0)
    by_lo = [lax.all_gather(pair[y], "x", axis=0, tiled=True) for y in range(2)]

    tile = jnp.concatenate([dot_nt(part, by_hi) for part in by_lo]) * (1.0 / N)
    gram = sum_pieces(tile.reshape(8, rows, 8 * rows), ("core", "y_hi"))

    rounded = gram.astype(jnp.bfloat16)
    right = spread(rounded, "z").reshape(8 * rows, 8 * rows)
    right_other = lax.ppermute(right, "core", [(0, 1), (1, 0)])
    left = lax.all_gather(swap_x_y_hi(rounded), "y_lo", axis=0)
    left = lax.all_gather(left, "x", axis=0).reshape(4, 2, rows, 8 * rows)
    core = lax.axis_index("core")
    own = jnp.where(core == 0, left[:, 0], left[:, 1]).reshape(4 * rows, 8 * rows)
    other = jnp.where(core == 0, left[:, 1], left[:, 0]).reshape(4 * rows, 8 * rows)
    square = jnp.dot(own, right, preferred_element_type=jnp.float32) + jnp.dot(
        other, right_other, preferred_element_type=jnp.float32
    )
    square = sum_pieces(square.reshape(4, rows, 8 * rows), "y_hi")

    place = (lax.axis_index("y_hi"), core, 0, 0)
    at_home = lax.dynamic_slice(left, place, (1, 1, rows, 8 * rows), allow_negative_indices=False)[0, 0]
    column = lax.broadcasted_iota(jnp.int32, at_home.shape, 1) - lax.axis_index("z") * rows
    on_diagonal = column == lax.broadcasted_iota(jnp.int32, at_home.shape, 0)
    diagonal = jnp.where(on_diagonal, at_home.astype(jnp.float32), 0.0).sum(1, keepdims=True)
    square = square + rest_of(gram) * (2.0 * diagonal)

    poly = (coef_cubic * gram + coef_quintic * square).astype(jnp.bfloat16)
    poly = lax.all_gather(spread(poly, "y_hi"), "core", axis=0).reshape(8 * rows, 8 * rows)
    product = jnp.dot(poly, by_hi, preferred_element_type=jnp.float32)
    mine = jnp.arange(8)[:, None, None] == lax.axis_index(("y_lo", "x"))
    linear = coef_linear * jnp.where(mine, x_scaled, 0.0)
    return sum_pieces(product.reshape(8, rows, cols) + linear, ("y_lo", "x"))


def solution(mesh):
    fine = Mesh(mesh.devices.reshape(2, 8, 4, 4, 2), MESH)
    return jax.shard_map(
        per_device,
        mesh=fine,
        in_specs=(P(ROW, COL),),
        out_specs=P(ROW, COL),
        check_vma=False,
    )
```
